256 devices in a mesh: visit: 16 (over y, x_lo, core), row: 16 (over z, x_hi).
Axes of the slice: x: 4 (x_hi: 2, x_lo: 2; x = x_hi * 2 + x_lo), y: 4, z: 8, core: 2. Of those that a mesh axis runs over, the one named last changes fastest.
Arguments:
- science: float32 [16, 512, 4096], P('visit', 'row'), may hold values from -8 to 8
- basis_kernels: float32 [9, 21, 21], replicated, may hold values from -0.25 to 0.25
- basis_coeffs: float32 [16, 9], P('visit'), may hold values from -2 to 2
- row_starts: int32 [16, 512], P('visit', 'row'), may hold values from -7 to 1
- row_taps: float32 [16, 8, 512], P('visit', None, 'row'), may hold values from -0.2 to 0.45
- col_offsets: int32 [16], P('visit'), may hold values from 0 to 511
- col_starts: int32 [16, 4096], P('visit'), may hold values from -3 to -2
- col_taps: float32 [16, 8, 4096], P('visit'), may hold values from -0.2 to 0.45
- visit_weights: float32 [16], P('visit'), may hold values from 0.25 to 4
- clip_masks: int32 [16, 512, 4096], P('visit', 'row'), may hold values 0 or 1
- decorrelation: float32 [16, 21, 21], P('visit'), may hold values from -0.25 to 0.25
Outputs:
- decorrelated: float32 [16, 512, 4096], P('visit', 'row')
- template: float32 [512, 4096], P('row', 'visit')
The draws below stay inside these ranges and needn't reach their ends.
Inputs may be any that keep to these rules, and one draw needn't show every extreme that they name: Row i of a visit reads matched rows i + row_starts[v, i] to i + row_starts[v, i] + 7.
All inputs are finite; a program needn't handle non-finite values. No bound on the sum of `clip_masks` on one device may be relied on, other than what follows from the above.
Results may differ from the reference program's by a relative error of at most 0.0003.
Values sent between devices are 32-bit elements; how exact they have to be, the bound alone decides.
No kernel may reach another device: no remote copies, remote signals or barrier semaphores. Data moves between devices by JAX's collectives and lax.ppermute only.
A program may use at most 64 MiB of HBM per device.

```python
import math
import jax
import jax.numpy as jnp
from jax import lax

W = 4096
KS = 21
NBASIS = 9
TAPS = 8
DITHER = 512
VISITS = 16
H = 512


def place_ends(entries, own_key, least, top_value):
    place = [jax.random.randint(jax.random.fold_in(own_key, axis), (), 0, length) for axis, length in enumerate(entries.shape)]
    main_axis = entries.shape.index(max(entries.shape))
    neighbour = place[:main_axis] + [(place[main_axis] + 1) % entries.shape[main_axis]] + place[main_axis + 1:]
    return entries.at[tuple(place)].set(least).at[tuple(neighbour)].set(top_value)


def block_levels(key, extent, split, smallest, top_value):
    level = 1.0
    for axis_at, shards_of in split:
        steps = jax.random.uniform(jax.random.fold_in(jax.random.fold_in(key, 6), axis_at), (shards_of,), jnp.float32, smallest / len(split), top_value / len(split))
        level = level * jnp.repeat(jnp.exp(steps), extent[axis_at] // shards_of).reshape((-1,) + (1,) * (len(extent) - 1 - axis_at))
    return level


def gaussian(own_key, dims, width, bound, split=(), kind=jnp.bfloat16):
    level = block_levels(own_key, dims, split, -0.22, 0.18) if split else 1.0
    drawn = jax.random.normal(own_key, dims, jnp.float32) * width * level
    return jnp.minimum(jnp.maximum(drawn, -bound), bound).astype(kind)


def setup_inputs(seed: int = 0) -> dict:
    keys = jax.random.split(jax.random.key(seed), 12)
    return {
        "science": gaussian(keys[0], (VISITS, H, W), 1.0, 8.0, ((0, 16), (1, 16)), jnp.float32),
        "basis_kernels": gaussian(keys[1], (NBASIS, KS, KS), (KS * KS) ** -0.5, 0.25, (), jnp.float32),
        "basis_coeffs": gaussian(keys[2], (VISITS, NBASIS), 0.33, 2.0, ((0, 16),), jnp.float32),
        "row_starts": place_ends(jax.random.randint(keys[3], (VISITS, H), -7, 2), jax.random.fold_in(keys[3], 1), -7, 1).astype(jnp.int32),
        "row_taps": jnp.clip(-0.2 + 0.65 * jax.random.uniform(keys[4], (VISITS, TAPS, H), jnp.float32) ** block_levels(keys[4], (VISITS, TAPS, H), ((0, 16), (2, 16)), -0.2, 0.2), -0.2, 0.45),
        "col_offsets": place_ends(jax.random.randint(keys[5], (VISITS,), 0, DITHER), jax.random.fold_in(keys[5], 1), 0, DITHER - 1).astype(jnp.int32),
        "col_starts": place_ends(jax.random.randint(keys[6], (VISITS, W), -3, -1), jax.random.fold_in(keys[6], 1), -3, (-1) - 1).astype(jnp.int32),
        "col_taps": jnp.clip(-0.2 + 0.65 * jax.random.uniform(keys[7], (VISITS, TAPS, W), jnp.float32) ** block_levels(keys[7], (VISITS, TAPS, W), ((0, 16),), -0.2, 0.2), -0.2, 0.45),
        "visit_weights": jnp.clip(jnp.exp(math.log(4.0) - 2.7725887 * jax.random.uniform(keys[8], (VISITS,), jnp.float32) ** block_levels(keys[8], (VISITS,), ((0, 16),), -0.2, 0.2)), 0.25, 4.0),
        "clip_masks": place_ends((jax.random.randint(keys[9], (VISITS, H, W), 0, 8) < 7).astype(jnp.int32), jax.random.fold_in(keys[9], 1), 0, 1),
        "decorrelation": gaussian(keys[10], (VISITS, KS, KS), (KS * KS) ** -0.5, 0.25, ((0, 16),), jnp.float32),
    }


def correlate(pixels, kernel):
    half_width = KS // 2
    result = lax.conv_general_dilated(pixels[None, None], kernel[None, None], (1, 1), ((half_width, half_width), (half_width, half_width)), precision=lax.Precision.HIGHEST)
    return result[0, 0]


def reference(science, basis_kernels, basis_coeffs, row_starts, row_taps, col_offsets, col_starts, col_taps, visit_weights, clip_masks, decorrelation):
    def warp_visit(operands):
        pixels, mixing, shift_rows, taps_rows, dither, shift_cols, taps_cols, weight_now, mask_now = operands
        kernel = jnp.einsum("b,bij->ij", mixing, basis_kernels, precision=lax.Precision.HIGHEST)
        matched = correlate(pixels, kernel)
        padded = jnp.pad(matched, ((TAPS, TAPS), (0, 0)))
        row_index = jnp.arange(H, dtype=jnp.int32) + shift_rows + TAPS
        rowwarp = jnp.zeros((H, W), jnp.float32)
        for tap_index in range(TAPS):
            rowwarp = rowwarp + taps_rows[tap_index][:, None] * jnp.take(padded, row_index + tap_index, axis=0)
        widened = jnp.pad(rowwarp, ((0, 0), (DITHER + 3, 8)))
        actual_start = jnp.arange(W, dtype=jnp.int32) - dither + shift_cols
        warped = jnp.zeros((H, W), jnp.float32)
        for tap_index in range(TAPS):
            warped = warped + taps_cols[tap_index][None, :] * jnp.take(widened, actual_start + DITHER + 3 + tap_index, axis=1)
        covered = ((actual_start >= 0) & (actual_start <= W - TAPS)).astype(jnp.float32)
        share = weight_now * mask_now.astype(jnp.float32) * covered[None, :]
        return warped, share

    warped, share = lax.map(warp_visit, (science, basis_coeffs, row_starts, row_taps, col_offsets, col_starts, col_taps, visit_weights, clip_masks))
    numerator = jnp.sum(share * warped, axis=0)
    denominator = jnp.sum(share, axis=0)
    template = numerator / jnp.maximum(denominator, 1.0)

    def clean_visit(operands):
        warped_now, kernel_now = operands
        return correlate(warped_now - template, kernel_now)

    decorrelated = lax.map(clean_visit, (warped, decorrelation))
    return decorrelated, template
```

```python
import jax
import jax.numpy as jnp
from jax import lax
from jax.experimental import pallas as pl
from jax.experimental.pallas import tpu as pltpu
from jax.sharding import PartitionSpec as P

KS = 21
HALF = KS // 2
TAPS = 8
ROWS = 32
COLS = 4096
BAND = 80
BASE = 24
LEAD = 6
CHUNK = 1024
BLOCK = 256
GROUP = 3
STEPS = KS // GROUP
FRAME = COLS + 128
LEFT = 640
F32 = jnp.float32
BF16 = jnp.bfloat16
VMEM_LIMIT = 48 * 1024 * 1024

VM = pl.BlockSpec(memory_space=pltpu.VMEM)
SM = pl.BlockSpec(memory_space=pltpu.SMEM)


def call(kernel, outs, ins, scratch=(), cost=None):
    return pl.pallas_call(
        kernel,
        out_shape=outs,
        in_specs=ins,
        out_specs=jax.tree.map(lambda _: VM, outs),
        scratch_shapes=list(scratch),
        compiler_params=pltpu.CompilerParams(vmem_limit_bytes=VMEM_LIMIT),
        cost_estimate=cost,
    )


def sds(*shape, dtype=F32):
    return jax.ShapeDtypeStruct(shape, dtype)


def pack_kernel(source_ref, up_ref, down_ref, x_ref, sem):
    fetch = pltpu.make_async_copy(source_ref, x_ref, sem)
    fetch.start()
    fetch.wait()
    for q in range(4):
        cols = pl.ds(q * CHUNK, CHUNK)
        down_ref[16 * q : 16 * q + 16, :] = x_ref[16:32, cols]
        up_ref[16 * q : 16 * q + 16, :] = x_ref[0:16, cols]
        down_ref[64 + q : 65 + q, :] = x_ref[15:16, cols]
        down_ref[68 + q : 69 + q, :] = jnp.zeros((1, CHUNK), F32)
        up_ref[64 + q : 65 + q, :] = x_ref[16:17, cols]
        up_ref[68 + q : 69 + q, :] = x_ref[17:18, cols]


def split_bands(values):
    lanes = lax.broadcasted_iota(jnp.int32, values.shape, 1)
    high = values.astype(BF16).astype(F32)
    return jnp.where(lanes < 2 * BAND, high, values - high).astype(BF16)


def bands_kernel(k1_ref, k2_ref, mix_ref, a1_ref, a2_ref):
    mix = mix_ref[...]
    for lag in range(KS):
        first = jnp.broadcast_to(k1_ref[lag : lag + 1, :], (48, 256))
        first = pltpu.roll(first, 0, 1, stride=1, stride_axis=0)
        merged = jnp.dot(
            mix, first, precision=lax.Precision.HIGHEST, preferred_element_type=F32
        )
        step, part = lag // GROUP, lag % GROUP
        rows, lanes = pl.ds(ROWS * step, ROWS), pl.ds(256 * part, 256)
        a1_ref[rows, lanes] = split_bands(merged)
        second = jnp.broadcast_to(k2_ref[lag : lag + 1, :], (ROWS, 256))
        second = pltpu.roll(second, 8, 1, stride=1, stride_axis=0)
        a2_ref[rows, lanes] = split_bands(second)


def coverage(starts, offset, q):
    column = lax.broadcasted_iota(jnp.int32, starts.shape, 1) + q * CHUNK
    actual = column - offset + starts
    return ((actual >= 0) & (actual <= COLS - TAPS)).astype(F32)


def put_blocks(ref, values, place_ref, q):
    core = place_ref[1]
    pair = place_ref[2]
    for j in range(4):
        ref[(j % 2) ^ core, (j // 2) ^ pair, q] = values[:, j * BLOCK : (j + 1) * BLOCK]


def share_kernel(place_ref, weight_ref, mask_ref, starts_ref, share_ref):
    for q in range(4):
        cols = pl.ds(q * CHUNK, CHUNK)
        covered = coverage(starts_ref[:, cols], place_ref[0], q)
        share = weight_ref[0] * mask_ref[:, cols].astype(F32) * covered
        put_blocks(share_ref, share, place_ref, q)


def put_rows(frame_ref, row, values, valid=None):
    count = values.shape[0]
    if valid is not None:
        values = jnp.where(valid, values, 0.0)
    framed = jnp.concatenate([values, jnp.zeros((count, 128), F32)], axis=1)
    frame_ref[row : row + count, :] = pltpu.roll(framed, HALF, 1)


def wide(ref, rows):
    return jnp.concatenate([ref[rows * q : rows * (q + 1), :] for q in range(4)], axis=1)


def thin(ref, at):
    return jnp.concatenate([ref[at + q : at + q + 1, :] for q in range(4)], axis=1)


def split_rows(frame_ref, halves_ref):
    frame = frame_ref[...]
    for part in range(GROUP):
        moved = pltpu.roll(frame, FRAME - part, 1) if part else frame
        high = moved.astype(BF16)
        at = 256 * part
        halves_ref[at : at + BAND, :] = high
        halves_ref[at + BAND : at + 2 * BAND, :] = (moved - high.astype(F32)).astype(BF16)
        halves_ref[at + 2 * BAND : at + 3 * BAND, :] = high
        halves_ref[at + 3 * BAND : at + 256, :] = jnp.zeros((256 - 3 * BAND, FRAME), BF16)


def correlate_chunk(band_ref, halves_ref, q):
    width = CHUNK + 128
    lags = jnp.dot(
        band_ref[...],
        halves_ref[:, q * CHUNK : q * CHUNK + width],
        preferred_element_type=F32,
    )
    total = lags[0:ROWS, :CHUNK]
    for step in range(1, STEPS):
        moved = pltpu.roll(lags[ROWS * step : ROWS * (step + 1), :], width - GROUP * step, 1)
        total = total + moved[:, :CHUNK]
    return total


def warp_kernel(
    place_ref,
    weight_ref,
    own_ref,
    above_ref,
    below_ref,
    band_ref,
    starts_ref,
    taps_ref,
    mask_ref,
    after_ref,
    warped_ref,
    weighted_ref,
    frame_ref,
    halves_ref,
    source_ref,
):
    band = place_ref[3]
    has_above, has_below = band > 0, band < 15
    put_rows(frame_ref, BASE, own_ref[...])
    put_rows(frame_ref, BASE - 16, wide(above_ref, 16), has_above)
    put_rows(frame_ref, BASE + ROWS, wide(below_ref, 16), has_below)
    frame_ref[0:8, :] = jnp.zeros((8, FRAME), F32)
    frame_ref[BAND - 8 : BAND, :] = jnp.zeros((8, FRAME), F32)
    put_rows(frame_ref, BASE - 17, thin(above_ref, 64), has_above)
    put_rows(frame_ref, BASE + 48, thin(below_ref, 64), has_below)
    put_rows(frame_ref, BASE + 49, thin(below_ref, 68), has_below)
    split_rows(frame_ref, halves_ref)

    source_ref[:, 0:LEFT] = jnp.zeros((ROWS, LEFT), F32)
    source_ref[:, LEFT + COLS : LEFT + COLS + 128] = jnp.zeros((ROWS, 128), F32)
    for q in range(4):
        source_ref[:, LEFT + q * CHUNK : LEFT + (q + 1) * CHUNK] = correlate_chunk(
            band_ref, halves_ref, q
        )

    offset = place_ref[0]
    first = LEFT - 3 - offset
    aligned = first // 128
    rest = first - aligned * 128
    width = CHUNK + 256
    for q in range(4):
        cols = pl.ds(q * CHUNK, CHUNK)
        at = pl.multiple_of((aligned + q * (CHUNK // 128)) * 128, 128)
        moved = pltpu.roll(source_ref[:, pl.ds(at, width)], width - rest, 1)
        starts = starts_ref[:, cols]
        early = starts == -3
        taps = [taps_ref[t : t + 1, cols] for t in range(TAPS)]
        zero = jnp.zeros_like(taps[0])
        total = None
        for lag in range(TAPS + 1):
            tap = jnp.where(
                early, taps[lag] if lag < TAPS else zero, taps[lag - 1] if lag else zero
            )
            part = moved if lag == 0 else pltpu.roll(moved, width - lag, 1)
            term = tap * part[:, :CHUNK]
            total = term if total is None else total + term
        warped_ref[:, cols] = total
        share = weight_ref[0] * mask_ref[:, cols].astype(F32) * coverage(starts, offset, q)
        put_blocks(weighted_ref, share * total, place_ref, q)


def differ_kernel(place_ref, own_ref, mine_ref, other_ref, diff_ref, up_ref, down_ref):
    core = place_ref[1]
    pair = place_ref[2]
    for b in range(16):
        cols = pl.ds(b * BLOCK, BLOCK)
        at = ((b // 2) % 2) ^ pair
        coadd = jnp.where(core == b % 2, mine_ref[at, b // 4], other_ref[at, b // 4])
        diff_ref[:, cols] = own_ref[:, cols] - coadd
    for q in range(4):
        cols = pl.ds(q * CHUNK, CHUNK)
        down_ref[8 * q : 8 * q + 8, :] = diff_ref[24:32, cols]
        up_ref[8 * q : 8 * q + 8, :] = diff_ref[0:8, cols]
        for extra in range(2):
            at = 32 + 4 * extra + q
            down_ref[at : at + 1, :] = diff_ref[22 + extra : 23 + extra, cols]
            up_ref[at : at + 1, :] = diff_ref[8 + extra : 9 + extra, cols]


def clean_kernel(
    place_ref, own_ref, above_ref, below_ref, band_ref, out_ref, frame_ref, halves_ref
):
    band = place_ref[3]
    has_above, has_below = band > 0, band < 15
    frame_ref[0:16, :] = jnp.zeros((16, FRAME), F32)
    frame_ref[BAND - 16 : BAND, :] = jnp.zeros((16, FRAME), F32)
    put_rows(frame_ref, BASE, own_ref[...])
    put_rows(frame_ref, BASE - 8, wide(above_ref, 8), has_above)
    put_rows(frame_ref, BASE + ROWS, wide(below_ref, 8), has_below)
    for extra in range(2):
        put_rows(frame_ref, BASE - 10 + extra, thin(above_ref, 32 + 4 * extra), has_above)
        put_rows(frame_ref, BASE + 40 + extra, thin(below_ref, 32 + 4 * extra), has_below)
    split_rows(frame_ref, halves_ref)
    for q in range(4):
        out_ref[:, q * CHUNK : (q + 1) * CHUNK] = correlate_chunk(band_ref, halves_ref, q)


def three_places(kernel):
    span = jnp.pad(kernel.T, ((0, 3), (LEAD, BAND - LEAD - KS)))
    return jnp.pad(jnp.concatenate([span] * 3, axis=1), ((0, 0), (0, 256 - 3 * BAND)))


def swap(values, step):
    return lax.ppermute(values, "visit", [(i, i ^ step) for i in range(16)])


RING_A = [(i, (i // 4 ^ 1) * 4 + i % 4) for i in range(16)]
RING_B = [(i, (3 - i // 4) * 4 + i % 4) for i in range(16)]


def over_y(part):
    part = part + lax.ppermute(part, "visit", RING_A)
    return part + lax.ppermute(part, "visit", RING_B)


def over_visits(blocks):
    half = blocks[0] + swap(blocks[1], 1)
    return over_y(half[0] + swap(half[1], 2))


def to_next(values):
    return lax.ppermute(values, "row", [(i, (i + 1) % 16) for i in range(16)])


def to_previous(values):
    return lax.ppermute(values, "row", [((i + 1) % 16, i) for i in range(16)])


def on_device(
    science,
    basis_kernels,
    basis_coeffs,
    row_starts,
    row_taps,
    col_offsets,
    col_starts,
    col_taps,
    visit_weights,
    clip_masks,
    decorrelation,
):
    pixels = science[0]
    visit = lax.axis_index("visit")
    band = lax.axis_index("row")
    band_at = band * ROWS
    place = jnp.stack([col_offsets[0], visit % 2, (visit // 2) % 2, band]).astype(jnp.int32)

    up, down = call(
        pack_kernel,
        (sds(72, CHUNK), sds(72, CHUNK)),
        [pl.BlockSpec(memory_space=pl.ANY)],
        [pltpu.VMEM((ROWS, COLS), F32), pltpu.SemaphoreType.DMA],
    )(pixels)
    above = to_next(down)
    below = to_previous(up)

    kernel = jnp.einsum(
        "b,bij->ij", basis_coeffs[0], basis_kernels, precision=lax.Precision.HIGHEST
    )
    matched_row = jnp.arange(48, dtype=jnp.int32)[None, :] - 8
    tap_at = matched_row - (jnp.arange(ROWS, dtype=jnp.int32) + row_starts[0])[:, None]
    inside = (matched_row + band_at >= 0) & (matched_row + band_at < 16 * ROWS)
    hits = tap_at[None] == jnp.arange(TAPS, dtype=jnp.int32)[:, None, None]
    mix = jnp.sum(jnp.where(hits & inside[None], row_taps[0][:, :, None], 0.0), axis=0)
    first_bands, second_bands = call(
        bands_kernel, (sds(STEPS * ROWS, GROUP * 256, dtype=BF16),) * 2, [VM] * 3
    )(three_places(kernel), three_places(decorrelation[0]), mix)

    shares = call(share_kernel, sds(2, 2, 4, ROWS, BLOCK), [SM, SM, VM, VM])(
        place, visit_weights, clip_masks[0], col_starts
    )
    shares = over_y(shares[0] + swap(shares[1], 1))
    denominator = jnp.maximum(shares[0] + swap(shares[1], 2), 1.0)

    frames = [
        pltpu.VMEM((BAND, FRAME), F32),
        pltpu.VMEM((GROUP * 256, FRAME), BF16),
    ]
    warped, weighted = call(
        warp_kernel,
        (sds(ROWS, COLS), sds(2, 2, 4, ROWS, BLOCK)),
        [SM, SM] + [VM] * 7 + [pl.BlockSpec(memory_space=pl.ANY)],
        frames + [pltpu.VMEM((ROWS, LEFT + COLS + 128), F32)],
    )(
        place,
        visit_weights,
        pixels,
        above,
        below,
        first_bands,
        col_starts,
        col_taps[0],
        clip_masks[0],
        shares,
    )
    weighted, denominator = lax.optimization_barrier((weighted, denominator))
    coadd = over_visits(weighted) / denominator
    template = lax.dynamic_index_in_dim(coadd, visit // 4, 0, keepdims=False)
    mine = jnp.stack([coadd, swap(coadd, 2)])
    other = swap(mine, 1)
    difference, up, down = call(
        differ_kernel,
        (sds(ROWS, COLS), sds(40, CHUNK), sds(40, CHUNK)),
        [SM] + [VM] * 3,
    )(place, warped, mine, other)
    cleaned = call(clean_kernel, sds(ROWS, COLS), [SM] + [VM] * 4, frames)(
        place, difference, to_next(down), to_previous(up), second_bands
    )
    return cleaned[None], template


def solution(mesh):
    return jax.shard_map(
        on_device,
        mesh=mesh,
        in_specs=(
            P("visit", "row", None),
            P(),
            P("visit", None),
            P("visit", "row"),
            P("visit", None, "row"),
            P("visit"),
            P("visit", None),
            P("visit", None, None),
            P("visit"),
            P("visit", "row", None),
            P("visit", None, None),
        ),
        out_specs=(P("visit", "row", None), P("row", "visit")),
        check_vma=False,
    )
```

```python
import jax
import jax.numpy as jnp
from jax import lax
from jax.experimental import pallas as pl
from jax.experimental.pallas import tpu as pltpu
from jax.sharding import PartitionSpec as P

KS = 21
HALF = KS // 2
TAPS = 8
ROWS = 32
COLS = 4096
SPAN = 40
SLOT = 128
BASE = 24
LEAD = 6
CHUNK = 1024
BLOCK = 256
GROUP = 4
STEPS = 6
FRAME = COLS + 128
LEFT = 640
F32 = jnp.float32
BF16 = jnp.bfloat16
VMEM_LIMIT = 16 * 1024 * 1024

VM = pl.BlockSpec(memory_space=pltpu.VMEM)
SM = pl.BlockSpec(memory_space=pltpu.SMEM)


def call(kernel, outs, ins, scratch=(), cost=None):
    return pl.pallas_call(
        kernel,
        out_shape=outs,
        in_specs=ins,
        out_specs=jax.tree.map(lambda _: VM, outs),
        scratch_shapes=list(scratch),
        compiler_params=pltpu.CompilerParams(vmem_limit_bytes=VMEM_LIMIT),
        cost_estimate=cost,
    )


def sds(*shape, dtype=F32):
    return jax.ShapeDtypeStruct(shape, dtype)


def pack_kernel(x_ref, up_ref, down_ref):
    for q in range(4):
        cols = pl.ds(q * CHUNK, CHUNK)
        down_ref[16 * q : 16 * q + 16, :] = x_ref[16:32, cols]
        up_ref[16 * q : 16 * q + 16, :] = x_ref[0:16, cols]
        down_ref[64 + q : 65 + q, :] = x_ref[15:16, cols]
        down_ref[68 + q : 69 + q, :] = jnp.zeros((1, CHUNK), F32)
        up_ref[64 + q : 65 + q, :] = x_ref[16:17, cols]
        up_ref[68 + q : 69 + q, :] = x_ref[17:18, cols]


def between(values, low, high, shift):
    lanes = lax.broadcasted_iota(jnp.int32, values.shape, 1)
    return pltpu.roll(jnp.where((lanes >= low) & (lanes < high), values, 0.0), shift % SLOT, 1)


def put_bands(ref, values):
    lanes = lax.broadcasted_iota(jnp.int32, values.shape, 1)
    spans = values + pltpu.roll(values, SPAN, 1) + pltpu.roll(values, 2 * SPAN, 1)
    high = spans.astype(BF16).astype(F32)
    parts = jnp.where(lanes < 2 * SPAN, high, spans - high).astype(BF16)
    for lag in range(GROUP * STEPS):
        rows = pl.ds(ROWS * (lag // GROUP), ROWS)
        slot = pl.ds(SLOT * (lag % GROUP), SLOT)
        ref[rows, slot] = parts[ROWS * lag : ROWS * (lag + 1)]


def put_both(own_ref, edge_ref, values):
    put_bands(own_ref, between(values, BASE, BASE + ROWS, -BASE))
    edge = between(values, BASE - 16, BASE, 16 - BASE)
    edge = edge + between(values, BASE + ROWS, BASE + ROWS + 18, 16 - BASE - ROWS)
    put_bands(edge_ref, edge + between(values, BASE - 17, BASE - 16, 39 - (BASE - 17)))


def skewed(ref, lag, rows, shift):
    values = jnp.broadcast_to(ref[lag : lag + 1, :], (rows, SLOT))
    return pltpu.roll(values, shift, 1, stride=1, stride_axis=0)


def bands_kernel(k1_ref, k2_ref, mix_ref, own1_ref, edge1_ref, own2_ref, edge2_ref):
    first = jnp.concatenate([skewed(k1_ref, lag, 48, 0) for lag in range(24)], axis=1)
    merged = jnp.dot(
        mix_ref[...], first, precision=lax.Precision.HIGHEST, preferred_element_type=F32
    )
    slots = [merged[:, SLOT * lag : SLOT * (lag + 1)] for lag in range(24)]
    put_both(own1_ref, edge1_ref, jnp.concatenate(slots, axis=0))
    slots = [skewed(k2_ref, lag, ROWS, 8) for lag in range(24)]
    put_both(own2_ref, edge2_ref, jnp.concatenate(slots, axis=0))


def coverage(starts, offset, q):
    column = lax.broadcasted_iota(jnp.int32, starts.shape, 1) + q * CHUNK
    actual = column - offset + starts
    return ((actual >= 0) & (actual <= COLS - TAPS)).astype(F32)


def put_blocks(ref, values, row, place_ref, q):
    for j in range(4):
        at = (j % 2) ^ place_ref[1], 2 * q + j // 2, pl.ds(row, ROWS)
        ref[at] = values[:, j * BLOCK : (j + 1) * BLOCK]


def clear(frame_ref, row):
    frame_ref[:, COLS:FRAME] = jnp.zeros((SPAN, FRAME - COLS), F32)
    frame_ref[row:SPAN, 0:COLS] = jnp.zeros((SPAN - row, COLS), F32)


def put_wide(frame_ref, row, ref, rows, valid):
    for q in range(4):
        values = jnp.where(valid, ref[rows * q : rows * (q + 1), :], 0.0)
        frame_ref[row : row + rows, q * CHUNK : (q + 1) * CHUNK] = values


def put_thin(frame_ref, row, ref, at, valid):
    for q in range(4):
        values = jnp.where(valid, ref[at + q : at + q + 1, :], 0.0)
        frame_ref[row : row + 1, q * CHUNK : (q + 1) * CHUNK] = values


def split_rows(frame_ref, halves_ref):
    frame = frame_ref[...]
    padding = jnp.zeros((SLOT - 3 * SPAN, FRAME), F32)
    for part in range(GROUP):
        moved = pltpu.roll(frame, HALF - part, 1)
        high = moved.astype(BF16).astype(F32)
        spans = jnp.concatenate([high, moved - high, high, padding], axis=0)
        halves_ref[SLOT * part : SLOT * (part + 1), :] = spans.astype(BF16)


def correlate_chunk(band_ref, halves_ref, q):
    width = CHUNK + 128
    lags = jnp.dot(
        band_ref[...],
        halves_ref[:, q * CHUNK : q * CHUNK + width],
        preferred_element_type=F32,
    )
    total = lags[0:ROWS, :CHUNK]
    for step in range(1, STEPS):
        moved = pltpu.roll(lags[ROWS * step : ROWS * (step + 1), :], width - GROUP * step, 1)
        total = total + moved[:, :CHUNK]
    return total


def own_kernel(own_ref, band_ref, out_ref, frame_ref, halves_ref):
    clear(frame_ref, ROWS)
    frame_ref[0:ROWS, 0:COLS] = own_ref[...]
    split_rows(frame_ref, halves_ref)
    for q in range(4):
        out_ref[:, q * CHUNK : (q + 1) * CHUNK] = correlate_chunk(band_ref, halves_ref, q)


def warp_kernel(
    place_ref,
    weight_ref,
    own_ref,
    above_ref,
    below_ref,
    band_ref,
    starts_ref,
    taps_ref,
    mask_ref,
    warped_ref,
    weighted_ref,
    frame_ref,
    halves_ref,
    source_ref,
):
    band = place_ref[2]
    has_above, has_below = band > 0, band < 15
    clear(frame_ref, 32)
    put_wide(frame_ref, 0, above_ref, 16, has_above)
    put_wide(frame_ref, 16, below_ref, 16, has_below)
    put_thin(frame_ref, 32, below_ref, 64, has_below)
    put_thin(frame_ref, 33, below_ref, 68, has_below)
    put_thin(frame_ref, 39, above_ref, 64, has_above)
    split_rows(frame_ref, halves_ref)

    source_ref[:, 0:LEFT] = jnp.zeros((ROWS, LEFT), F32)
    source_ref[:, LEFT + COLS : LEFT + COLS + 128] = jnp.zeros((ROWS, 128), F32)
    for q in range(4):
        edges = correlate_chunk(band_ref, halves_ref, q)
        source_ref[:, LEFT + q * CHUNK : LEFT + (q + 1) * CHUNK] = (
            own_ref[:, q * CHUNK : (q + 1) * CHUNK] + edges
        )

    offset = place_ref[0]
    first = LEFT - 3 - offset
    aligned = first // 128
    rest = first - aligned * 128
    width = CHUNK + 256
    for q in range(4):
        cols = pl.ds(q * CHUNK, CHUNK)
        at = pl.multiple_of((aligned + q * (CHUNK // 128)) * 128, 128)
        moved = pltpu.roll(source_ref[:, pl.ds(at, width)], width - rest, 1)
        starts = starts_ref[:, cols]
        early = starts == -3
        taps = [taps_ref[t : t + 1, cols] for t in range(TAPS)]
        zero = jnp.zeros_like(taps[0])
        total = None
        for lag in range(TAPS + 1):
            tap = jnp.where(
                early, taps[lag] if lag < TAPS else zero, taps[lag - 1] if lag else zero
            )
            part = moved if lag == 0 else pltpu.roll(moved, width - lag, 1)
            term = tap * part[:, :CHUNK]
            total = term if total is None else total + term
        warped_ref[:, cols] = total
        share = weight_ref[0] * mask_ref[:, cols].astype(F32) * coverage(starts, offset, q)
        put_blocks(weighted_ref, share * total, 0, place_ref, q)
        put_blocks(weighted_ref, share, ROWS, place_ref, q)


def differ_kernel(
    place_ref,
    own_ref,
    mine_ref,
    other_ref,
    diff_ref,
    up_ref,
    down_ref,
):
    core = place_ref[1]
    for b in range(16):
        cols = pl.ds(b * BLOCK, BLOCK)
        coadd = jnp.where(core == b % 2, mine_ref[b // 2], other_ref[b // 2])
        diff_ref[:, cols] = own_ref[:, cols] - coadd
    for q in range(4):
        cols = pl.ds(q * CHUNK, CHUNK)
        down_ref[8 * q : 8 * q + 8, :] = diff_ref[24:32, cols]
        up_ref[8 * q : 8 * q + 8, :] = diff_ref[0:8, cols]
        for extra in range(2):
            at = 32 + 4 * extra + q
            down_ref[at : at + 1, :] = diff_ref[22 + extra : 23 + extra, cols]
            up_ref[at : at + 1, :] = diff_ref[8 + extra : 9 + extra, cols]


def clean_kernel(
    place_ref,
    own_ref,
    above_ref,
    below_ref,
    coadd_ref,
    band_ref,
    out_ref,
    template_ref,
    frame_ref,
    halves_ref,
):
    template_ref[...] = coadd_ref[...]
    band = place_ref[2]
    has_above, has_below = band > 0, band < 15
    clear(frame_ref, 0)
    put_wide(frame_ref, 8, above_ref, 8, has_above)
    put_wide(frame_ref, 16, below_ref, 8, has_below)
    for extra in range(2):
        put_thin(frame_ref, 6 + extra, above_ref, 32 + 4 * extra, has_above)
        put_thin(frame_ref, 24 + extra, below_ref, 32 + 4 * extra, has_below)
    split_rows(frame_ref, halves_ref)
    for q in range(4):
        cols = pl.ds(q * CHUNK, CHUNK)
        out_ref[:, cols] = own_ref[:, cols] + correlate_chunk(band_ref, halves_ref, q)


def by_lag(kernel):
    return jnp.pad(kernel.T, ((0, 3), (LEAD, SLOT - LEAD - KS)))


def swap(values, step):
    return lax.ppermute(values, "visit", [(i, i ^ step) for i in range(16)])


def over_chips(blocks):
    return lax.all_to_all(
        blocks,
        "visit",
        split_axis=0,
        concat_axis=0,
        axis_index_groups=[list(range(core, 16, 2)) for core in range(2)],
        tiled=True,
    )


def to_next(values):
    return lax.ppermute(values, "row", [(i, (i + 1) % 16) for i in range(16)])


def to_previous(values):
    return lax.ppermute(values, "row", [((i + 1) % 16, i) for i in range(16)])


def on_device(
    science,
    basis_kernels,
    basis_coeffs,
    row_starts,
    row_taps,
    col_offsets,
    col_starts,
    col_taps,
    visit_weights,
    clip_masks,
    decorrelation,
):
    pixels = science[0]
    visit = lax.axis_index("visit")
    band = lax.axis_index("row")
    band_at = band * ROWS
    place = jnp.stack([col_offsets[0], visit % 2, band]).astype(jnp.int32)

    up, down = call(pack_kernel, (sds(72, CHUNK), sds(72, CHUNK)), [VM])(pixels)
    above = to_next(down)
    below = to_previous(up)

    kernel = jnp.einsum(
        "b,bij->ij", basis_coeffs[0], basis_kernels, precision=lax.Precision.HIGHEST
    )
    matched_row = jnp.arange(48, dtype=jnp.int32)[None, :] - 8
    tap_at = matched_row - (jnp.arange(ROWS, dtype=jnp.int32) + row_starts[0])[:, None]
    inside = (matched_row + band_at >= 0) & (matched_row + band_at < 16 * ROWS)
    hits = tap_at[None] == jnp.arange(TAPS, dtype=jnp.int32)[:, None, None]
    mix = jnp.sum(jnp.where(hits & inside[None], row_taps[0][:, :, None], 0.0), axis=0)
    own_first, edge_first, own_second, edge_second = call(
        bands_kernel, (sds(STEPS * ROWS, GROUP * SLOT, dtype=BF16),) * 4, [VM] * 3
    )(by_lag(kernel), by_lag(decorrelation[0]), mix)

    frames = [
        pltpu.VMEM((SPAN, FRAME), F32),
        pltpu.VMEM((GROUP * SLOT, FRAME), BF16),
    ]
    own_part = call(own_kernel, sds(ROWS, COLS), [VM] * 2, frames)(pixels, own_first)
    warped, weighted = call(
        warp_kernel,
        (sds(ROWS, COLS), sds(2, 8, 2 * ROWS, BLOCK)),
        [SM, SM] + [VM] * 7,
        frames + [pltpu.VMEM((ROWS, LEFT + COLS + 128), F32)],
    )(
        place,
        visit_weights,
        own_part,
        above,
        below,
        edge_first,
        col_starts,
        col_taps[0],
        clip_masks[0],
    )
    half = weighted[0] + swap(weighted[1], 1)
    total = jnp.sum(over_chips(half), axis=0)
    coadd = total[:ROWS] / jnp.maximum(total[ROWS:], 1.0)
    mine = over_chips(jnp.broadcast_to(coadd[None], (8, ROWS, BLOCK)))
    other = swap(mine, 1)
    difference, up, down = call(
        differ_kernel,
        (sds(ROWS, COLS), sds(40, CHUNK), sds(40, CHUNK)),
        [SM] + [VM] * 3,
    )(place, warped, mine, other)
    above, below = to_next(down), to_previous(up)
    own_part = call(own_kernel, sds(ROWS, COLS), [VM] * 2, frames)(difference, own_second)
    cleaned, template = call(
        clean_kernel, (sds(ROWS, COLS), sds(ROWS, BLOCK)), [SM] + [VM] * 5, frames
    )(place, own_part, above, below, coadd, edge_second)
    return cleaned[None], template


def solution(mesh):
    return jax.shard_map(
        on_device,
        mesh=mesh,
        in_specs=(
            P("visit", "row", None),
            P(),
            P("visit", None),
            P("visit", "row"),
            P("visit", None, "row"),
            P("visit"),
            P("visit", None),
            P("visit", None, None),
            P("visit"),
            P("visit", "row", None),
            P("visit", None, None),
        ),
        out_specs=(P("visit", "row", None), P("row", "visit")),
        check_vma=False,
    )
```

```python
import jax
import jax.numpy as jnp
from jax import lax
from jax.experimental import pallas as pl
from jax.experimental.pallas import tpu as pltpu
from jax.sharding import PartitionSpec as P

KS = 21
HALF = KS // 2
TAPS = 8
ROWS = 32
COLS = 4096
SPAN = 40
SLOT = 128
BASE = 24
LEAD = 6
CHUNK = 1024
BLOCK = 256
GROUP = 4
STEPS = 6
THIN = 16
THIN_GROUP = 5
THIN_STEPS = 5
FRAME = COLS + 128
LEFT = 640
F32 = jnp.float32
BF16 = jnp.bfloat16
VMEM_LIMIT = 16 * 1024 * 1024

VM = pl.BlockSpec(memory_space=pltpu.VMEM)
SM = pl.BlockSpec(memory_space=pltpu.SMEM)


ANY = pl.BlockSpec(memory_space=pl.ANY)


def call(kernel, outs, ins, scratch=(), places=None, aliases=None):
    return pl.pallas_call(
        kernel,
        out_shape=outs,
        in_specs=ins,
        out_specs=jax.tree.map(lambda _: VM, outs) if places is None else places,
        scratch_shapes=list(scratch),
        input_output_aliases=aliases or {},
        compiler_params=pltpu.CompilerParams(vmem_limit_bytes=VMEM_LIMIT),
    )


def sds(*shape, dtype=F32):
    return jax.ShapeDtypeStruct(shape, dtype)


def down_kernel(x_ref, down_ref):
    for q in range(4):
        cols = pl.ds(q * CHUNK, CHUNK)
        down_ref[16 * q : 16 * q + 16, :] = x_ref[16:32, cols]
        down_ref[64 + q : 65 + q, :] = x_ref[15:16, cols]
        down_ref[68 + q : 69 + q, :] = jnp.zeros((1, CHUNK), F32)


def up_kernel(x_ref, up_ref):
    for q in range(4):
        cols = pl.ds(q * CHUNK, CHUNK)
        up_ref[16 * q : 16 * q + 16, :] = x_ref[0:16, cols]
        up_ref[64 + q : 65 + q, :] = x_ref[16:17, cols]
        up_ref[68 + q : 69 + q, :] = x_ref[17:18, cols]


def between(values, low, high, shift):
    lanes = lax.broadcasted_iota(jnp.int32, values.shape, 1)
    return pltpu.roll(jnp.where((lanes >= low) & (lanes < high), values, 0.0), shift % SLOT, 1)


def put_bands(ref, values):
    lanes = lax.broadcasted_iota(jnp.int32, values.shape, 1)
    spans = values + pltpu.roll(values, SPAN, 1) + pltpu.roll(values, 2 * SPAN, 1)
    high = spans.astype(BF16).astype(F32)
    parts = jnp.where(lanes < 2 * SPAN, high, spans - high).astype(BF16)
    for lag in range(GROUP * STEPS):
        rows = pl.ds(ROWS * (lag // GROUP), ROWS)
        slot = pl.ds(SLOT * (lag % GROUP), SLOT)
        ref[rows, slot] = parts[ROWS * lag : ROWS * (lag + 1)]


def put_thin_bands(ref, values, low, row, valid):
    lanes = lax.broadcasted_iota(jnp.int32, values.shape, 1)
    span = jnp.where(valid, between(values, low, low + THIN, -low), 0.0)
    spans = span + pltpu.roll(span, THIN, 1) + pltpu.roll(span, 2 * THIN, 1)
    high = spans.astype(BF16).astype(F32)
    parts = jnp.where(lanes < 2 * THIN, high, spans - high)
    total = None
    for part in range(THIN_GROUP):
        rows = []
        for step in range(THIN_STEPS):
            at = ROWS * (THIN_GROUP * step + part) + row
            known = at < values.shape[0]
            rows.append(parts[at : at + THIN] if known else jnp.zeros((THIN, SLOT), F32))
        stacked = jnp.concatenate(rows, axis=0)
        wide = jnp.concatenate([stacked, jnp.zeros_like(stacked)], axis=1)
        moved = pltpu.roll(wide, 3 * THIN * part, 1) if part else wide
        total = moved if total is None else total + moved
    ref[...] = total.astype(BF16)


def put_both(own_ref, edge_ref, values, has_above, has_below):
    put_bands(own_ref, between(values, BASE, BASE + ROWS, -BASE))
    above = between(values, BASE - 16, BASE, 16 - BASE)
    above = above + between(values, BASE - 17, BASE - 16, 39 - (BASE - 17))
    below = between(values, BASE + ROWS, BASE + ROWS + 18, 16 - BASE - ROWS)
    put_bands(edge_ref, jnp.where(has_above, above, 0.0) + jnp.where(has_below, below, 0.0))


def skewed(ref, lag, rows, shift):
    values = jnp.broadcast_to(ref[lag : lag + 1, :], (rows, SLOT))
    return pltpu.roll(values, shift, 1, stride=1, stride_axis=0)


def bands_kernel(
    place_ref, k1_ref, k2_ref, mix_ref, own1_ref, edge1_ref, own2_ref, above2_ref, below2_ref
):
    has_above, has_below = place_ref[2] > 0, place_ref[2] < 15
    first = jnp.concatenate([skewed(k1_ref, lag, 48, 0) for lag in range(24)], axis=1)
    merged = jnp.dot(
        mix_ref[...], first, precision=lax.Precision.HIGHEST, preferred_element_type=F32
    )
    slots = [merged[:, SLOT * lag : SLOT * (lag + 1)] for lag in range(24)]
    put_both(own1_ref, edge1_ref, jnp.concatenate(slots, axis=0), has_above, has_below)
    slots = [skewed(k2_ref, lag, ROWS, 8) for lag in range(24)]
    values = jnp.concatenate(slots, axis=0)
    put_bands(own2_ref, between(values, BASE, BASE + ROWS, -BASE))
    put_thin_bands(above2_ref, values, BASE - THIN, 0, has_above)
    put_thin_bands(below2_ref, values, BASE + ROWS, ROWS - THIN, has_below)


def coverage(starts, offset, q):
    column = lax.broadcasted_iota(jnp.int32, starts.shape, 1) + q * CHUNK
    actual = column - offset + starts
    return ((actual >= 0) & (actual <= COLS - TAPS)).astype(F32)


def put_blocks(ref, values, row, place_ref, q):
    for j in range(4):
        at = (j % 2) ^ place_ref[1], 2 * q + j // 2, pl.ds(row, ROWS)
        ref[at] = values[:, j * BLOCK : (j + 1) * BLOCK]


def clear(frame_ref, row):
    rows = frame_ref.shape[0]
    frame_ref[:, COLS:FRAME] = jnp.zeros((rows, FRAME - COLS), F32)
    frame_ref[row:rows, 0:COLS] = jnp.zeros((rows - row, COLS), F32)


def put_wide(frame_ref, row, ref, rows):
    for q in range(4):
        cols = pl.ds(q * CHUNK, CHUNK)
        frame_ref[row : row + rows, cols] = ref[rows * q : rows * (q + 1), :]


def put_thin(frame_ref, row, ref, at):
    for q in range(4):
        frame_ref[row : row + 1, q * CHUNK : (q + 1) * CHUNK] = ref[at + q : at + q + 1, :]


def split_rows(frame_ref, halves_ref):
    frame = frame_ref[...]
    padding = jnp.zeros((SLOT - 3 * SPAN, FRAME), F32)
    for part in range(GROUP):
        moved = pltpu.roll(frame, HALF - part, 1)
        high = moved.astype(BF16).astype(F32)
        spans = jnp.concatenate([high, moved - high, high, padding], axis=0)
        halves_ref[SLOT * part : SLOT * (part + 1), :] = spans.astype(BF16)


def correlate_chunk(band_ref, halves_ref, q):
    width = CHUNK + 128
    lags = jnp.dot(
        band_ref[...],
        halves_ref[:, q * CHUNK : q * CHUNK + width],
        preferred_element_type=F32,
    )
    total = lags[0:ROWS, :CHUNK]
    for step in range(1, STEPS):
        moved = pltpu.roll(lags[ROWS * step : ROWS * (step + 1), :], width - GROUP * step, 1)
        total = total + moved[:, :CHUNK]
    return total


def own_kernel(own_ref, band_ref, out_ref, frame_ref, halves_ref):
    clear(frame_ref, ROWS)
    frame_ref[0:ROWS, 0:COLS] = own_ref[...]
    split_rows(frame_ref, halves_ref)
    for q in range(4):
        out_ref[:, q * CHUNK : (q + 1) * CHUNK] = correlate_chunk(band_ref, halves_ref, q)


def warp_kernel(
    place_ref,
    weight_ref,
    own_ref,
    above_ref,
    below_ref,
    band_ref,
    starts_ref,
    taps_ref,
    mask_ref,
    warped_ref,
    weighted_ref,
    frame_ref,
    halves_ref,
    source_ref,
):
    clear(frame_ref, 32)
    put_wide(frame_ref, 0, above_ref, 16)
    put_wide(frame_ref, 16, below_ref, 16)
    put_thin(frame_ref, 32, below_ref, 64)
    put_thin(frame_ref, 33, below_ref, 68)
    put_thin(frame_ref, 39, above_ref, 64)
    split_rows(frame_ref, halves_ref)

    source_ref[:, 0:LEFT] = jnp.zeros((ROWS, LEFT), F32)
    source_ref[:, LEFT + COLS : LEFT + COLS + 128] = jnp.zeros((ROWS, 128), F32)
    for q in range(4):
        edges = correlate_chunk(band_ref, halves_ref, q)
        source_ref[:, LEFT + q * CHUNK : LEFT + (q + 1) * CHUNK] = (
            own_ref[:, q * CHUNK : (q + 1) * CHUNK] + edges
        )

    offset = place_ref[0]
    first = LEFT - 3 - offset
    aligned = first // 128
    rest = first - aligned * 128
    width = CHUNK + 256
    for q in range(4):
        cols = pl.ds(q * CHUNK, CHUNK)
        at = pl.multiple_of((aligned + q * (CHUNK // 128)) * 128, 128)
        moved = pltpu.roll(source_ref[:, pl.ds(at, width)], width - rest, 1)
        starts = starts_ref[:, cols]
        early = starts == -3
        taps = [taps_ref[t : t + 1, cols] for t in range(TAPS)]
        zero = jnp.zeros_like(taps[0])
        total = None
        for lag in range(TAPS + 1):
            tap = jnp.where(
                early, taps[lag] if lag < TAPS else zero, taps[lag - 1] if lag else zero
            )
            part = moved if lag == 0 else pltpu.roll(moved, width - lag, 1)
            term = tap * part[:, :CHUNK]
            total = term if total is None else total + term
        warped_ref[:, cols] = total
        share = weight_ref[0] * mask_ref[:, cols].astype(F32) * coverage(starts, offset, q)
        put_blocks(weighted_ref, share * total, 0, place_ref, q)
        put_blocks(weighted_ref, share, ROWS, place_ref, q)


def differ_kernel(
    place_ref,
    own_ref,
    mine_ref,
    other_ref,
    diff_ref,
    up_ref,
    down_ref,
):
    core = place_ref[1]
    for b in range(16):
        cols = pl.ds(b * BLOCK, BLOCK)
        coadd = jnp.where(core == b % 2, mine_ref[b // 2], other_ref[b // 2])
        diff_ref[:, cols] = own_ref[:, cols] - coadd
    for q in range(4):
        cols = pl.ds(q * CHUNK, CHUNK)
        down_ref[8 * q : 8 * q + 8, :] = diff_ref[24:32, cols]
        up_ref[8 * q : 8 * q + 8, :] = diff_ref[0:8, cols]
        for extra in range(2):
            at = 32 + 4 * extra + q
            down_ref[at : at + 1, :] = diff_ref[22 + extra : 23 + extra, cols]
            up_ref[at : at + 1, :] = diff_ref[8 + extra : 9 + extra, cols]


def thin_edges(own_ref, row, band_ref, out_ref, frame_ref, halves_ref, done_ref, sems):
    frame = frame_ref[...]
    for part in range(THIN_GROUP):
        moved = pltpu.roll(frame, HALF - part, 1)
        high = moved.astype(BF16).astype(F32)
        spans = jnp.concatenate([high, moved - high, high], axis=0)
        halves_ref[3 * THIN * part : 3 * THIN * (part + 1), :] = spans.astype(BF16)
    used = 3 * THIN * THIN_GROUP
    halves_ref[used:256, :] = jnp.zeros((256 - used, FRAME), BF16)
    width = CHUNK + 128
    copies = []
    for q in range(4):
        cols = pl.ds(q * CHUNK, CHUNK)
        lags = jnp.dot(
            band_ref[...],
            halves_ref[:, q * CHUNK : q * CHUNK + width],
            preferred_element_type=F32,
        )
        total = own_ref[row : row + THIN, cols] + lags[0:THIN, :CHUNK]
        for step in range(1, THIN_STEPS):
            lag = lags[THIN * step : THIN * (step + 1), :]
            total = total + pltpu.roll(lag, width - THIN_GROUP * step, 1)[:, :CHUNK]
        done_ref[:, cols] = total
        copy = pltpu.make_async_copy(
            done_ref.at[:, cols], out_ref.at[pl.ds(row, THIN), cols], sems.at[q]
        )
        copy.start()
        copies.append(copy)
    for copy in copies:
        copy.wait()


def above_kernel(
    own_ref,
    above_ref,
    coadd_ref,
    band_ref,
    out_ref,
    template_ref,
    frame_ref,
    halves_ref,
    done_ref,
    sems,
):
    template_ref[...] = coadd_ref[...]
    clear(frame_ref, 0)
    put_wide(frame_ref, 8, above_ref, 8)
    for extra in range(2):
        put_thin(frame_ref, 6 + extra, above_ref, 32 + 4 * extra)
    thin_edges(own_ref, 0, band_ref, out_ref, frame_ref, halves_ref, done_ref, sems)


def below_kernel(
    own_ref,
    below_ref,
    band_ref,
    begun_ref,
    out_ref,
    frame_ref,
    halves_ref,
    done_ref,
    sems,
):
    clear(frame_ref, 0)
    put_wide(frame_ref, 0, below_ref, 8)
    for extra in range(2):
        put_thin(frame_ref, 8 + extra, below_ref, 32 + 4 * extra)
    row = ROWS - THIN
    thin_edges(own_ref, row, band_ref, out_ref, frame_ref, halves_ref, done_ref, sems)


def by_lag(kernel):
    return jnp.pad(kernel.T, ((0, 3), (LEAD, SLOT - LEAD - KS)))


def swap(values, step):
    return lax.ppermute(values, "visit", [(i, i ^ step) for i in range(16)])


def over_chips(blocks):
    return lax.all_to_all(
        blocks,
        "visit",
        split_axis=0,
        concat_axis=0,
        axis_index_groups=[list(range(core, 16, 2)) for core in range(2)],
        tiled=True,
    )


def to_next(values):
    return lax.ppermute(values, "row", [(i, (i + 1) % 16) for i in range(16)])


def to_previous(values):
    return lax.ppermute(values, "row", [((i + 1) % 16, i) for i in range(16)])


def on_device(
    science,
    basis_kernels,
    basis_coeffs,
    row_starts,
    row_taps,
    col_offsets,
    col_starts,
    col_taps,
    visit_weights,
    clip_masks,
    decorrelation,
):
    pixels = science[0]
    visit = lax.axis_index("visit")
    band = lax.axis_index("row")
    band_at = band * ROWS
    place = jnp.stack([col_offsets[0], visit % 2, band]).astype(jnp.int32)

    above = to_next(call(down_kernel, sds(72, CHUNK), [VM])(pixels))
    below = to_previous(call(up_kernel, sds(72, CHUNK), [VM])(pixels))

    kernel = jnp.einsum(
        "b,bij->ij", basis_coeffs[0], basis_kernels, precision=lax.Precision.HIGHEST
    )
    matched_row = jnp.arange(48, dtype=jnp.int32)[None, :] - 8
    tap_at = matched_row - (jnp.arange(ROWS, dtype=jnp.int32) + row_starts[0])[:, None]
    inside = (matched_row + band_at >= 0) & (matched_row + band_at < 16 * ROWS)
    hits = tap_at[None] == jnp.arange(TAPS, dtype=jnp.int32)[:, None, None]
    mix = jnp.sum(jnp.where(hits & inside[None], row_taps[0][:, :, None], 0.0), axis=0)
    bands = sds(STEPS * ROWS, GROUP * SLOT, dtype=BF16)
    thin_bands = sds(THIN_STEPS * THIN, 256, dtype=BF16)
    own_first, edge_first, own_second, above_second, below_second = call(
        bands_kernel, (bands, bands, bands, thin_bands, thin_bands), [SM] + [VM] * 3
    )(place, by_lag(kernel), by_lag(decorrelation[0]), mix)

    frames = [
        pltpu.VMEM((SPAN, FRAME), F32),
        pltpu.VMEM((GROUP * SLOT, FRAME), BF16),
    ]
    own_part = call(own_kernel, sds(ROWS, COLS), [VM] * 2, frames)(pixels, own_first)
    warped, weighted = call(
        warp_kernel,
        (sds(ROWS, COLS), sds(2, 8, 2 * ROWS, BLOCK)),
        [SM, SM] + [VM] * 7,
        frames + [pltpu.VMEM((ROWS, LEFT + COLS + 128), F32)],
    )(
        place,
        visit_weights,
        own_part,
        above,
        below,
        edge_first,
        col_starts,
        col_taps[0],
        clip_masks[0],
    )
    half = weighted[0] + swap(weighted[1], 1)
    total = jnp.sum(over_chips(half), axis=0)
    coadd = total[:ROWS] / jnp.maximum(total[ROWS:], 1.0)
    mine = over_chips(jnp.broadcast_to(coadd[None], (8, ROWS, BLOCK)))
    other = swap(mine, 1)
    difference, up, down = call(
        differ_kernel,
        (sds(ROWS, COLS), sds(40, CHUNK), sds(40, CHUNK)),
        [SM] + [VM] * 3,
    )(place, warped, mine, other)
    above, below = to_next(down), to_previous(up)
    own_part = call(own_kernel, sds(ROWS, COLS), [VM] * 2, frames)(difference, own_second)
    thin_frames = [
        pltpu.VMEM((THIN, FRAME), F32),
        pltpu.VMEM((256, FRAME), BF16),
        pltpu.VMEM((THIN, COLS), F32),
        pltpu.SemaphoreType.DMA((4,)),
    ]
    begun, template = call(
        above_kernel,
        (sds(ROWS, COLS), sds(ROWS, BLOCK)),
        [VM] * 4,
        thin_frames,
        (ANY, VM),
    )(own_part, above, coadd, above_second)
    cleaned = call(
        below_kernel, sds(ROWS, COLS), [VM] * 3 + [ANY], thin_frames, ANY, {3: 0}
    )(own_part, below, below_second, begun)
    return cleaned[None], template


def solution(mesh):
    return jax.shard_map(
        on_device,
        mesh=mesh,
        in_specs=(
            P("visit", "row", None),
            P(),
            P("visit", None),
            P("visit", "row"),
            P("visit", None, "row"),
            P("visit"),
            P("visit", None),
            P("visit", None, None),
            P("visit"),
            P("visit", "row", None),
            P("visit", None, None),
        ),
        out_specs=(P("visit", "row", None), P("row", "visit")),
        check_vma=False,
    )
```

```python
import jax
import jax.numpy as jnp
from jax import lax
from jax.experimental import pallas as pl
from jax.experimental.pallas import tpu as pltpu
from jax.sharding import PartitionSpec as P

KS = 21
HALF = KS // 2
TAPS = 8
ROWS = 32
COLS = 4096
SPAN = 40
SLOT = 128
BASE = 24
LEAD = 6
CHUNK = 1024
BLOCK = 256
GROUP = 4
STEPS = 6
THIN = 16
THIN_GROUP = 5
THIN_STEPS = 5
FRAME = COLS + 128
LEFT = 640
F32 = jnp.float32
BF16 = jnp.bfloat16
VMEM_LIMIT = 16 * 1024 * 1024

VM = pl.BlockSpec(memory_space=pltpu.VMEM)
SM = pl.BlockSpec(memory_space=pltpu.SMEM)


ANY = pl.BlockSpec(memory_space=pl.ANY)


def call(kernel, outs, ins, scratch=(), places=None, aliases=None):
    return pl.pallas_call(
        kernel,
        out_shape=outs,
        in_specs=ins,
        out_specs=jax.tree.map(lambda _: VM, outs) if places is None else places,
        scratch_shapes=list(scratch),
        input_output_aliases=aliases or {},
        compiler_params=pltpu.CompilerParams(vmem_limit_bytes=VMEM_LIMIT),
    )


def sds(*shape, dtype=F32):
    return jax.ShapeDtypeStruct(shape, dtype)


def down_kernel(x_ref, down_ref):
    for q in range(4):
        cols = pl.ds(q * CHUNK, CHUNK)
        down_ref[16 * q : 16 * q + 16, :] = x_ref[16:32, cols]
        down_ref[64 + q : 65 + q, :] = x_ref[15:16, cols]
        down_ref[68 + q : 69 + q, :] = jnp.zeros((1, CHUNK), F32)


def up_kernel(x_ref, up_ref):
    for q in range(4):
        cols = pl.ds(q * CHUNK, CHUNK)
        up_ref[16 * q : 16 * q + 16, :] = x_ref[0:16, cols]
        up_ref[64 + q : 65 + q, :] = x_ref[16:17, cols]
        up_ref[68 + q : 69 + q, :] = x_ref[17:18, cols]


def between(values, low, high, shift):
    lanes = lax.broadcasted_iota(jnp.int32, values.shape, 1)
    return pltpu.roll(jnp.where((lanes >= low) & (lanes < high), values, 0.0), shift % SLOT, 1)


def put_bands(ref, values):
    lanes = lax.broadcasted_iota(jnp.int32, values.shape, 1)
    spans = values + pltpu.roll(values, SPAN, 1) + pltpu.roll(values, 2 * SPAN, 1)
    high = spans.astype(BF16).astype(F32)
    parts = jnp.where(lanes < 2 * SPAN, high, spans - high).astype(BF16)
    for lag in range(GROUP * STEPS):
        rows = pl.ds(ROWS * (lag // GROUP), ROWS)
        slot = pl.ds(SLOT * (lag % GROUP), SLOT)
        ref[rows, slot] = parts[ROWS * lag : ROWS * (lag + 1)]


def put_thin_bands(ref, values, low, row, valid):
    lanes = lax.broadcasted_iota(jnp.int32, values.shape, 1)
    span = jnp.where(valid, between(values, low, low + THIN, -low), 0.0)
    spans = span + pltpu.roll(span, THIN, 1) + pltpu.roll(span, 2 * THIN, 1)
    high = spans.astype(BF16).astype(F32)
    parts = jnp.where(lanes < 2 * THIN, high, spans - high)
    total = None
    for part in range(THIN_GROUP):
        rows = []
        for step in range(THIN_STEPS):
            at = ROWS * (THIN_GROUP * step + part) + row
            known = at < values.shape[0]
            rows.append(parts[at : at + THIN] if known else jnp.zeros((THIN, SLOT), F32))
        stacked = jnp.concatenate(rows, axis=0)
        wide = jnp.concatenate([stacked, jnp.zeros_like(stacked)], axis=1)
        moved = pltpu.roll(wide, 3 * THIN * part, 1) if part else wide
        total = moved if total is None else total + moved
    ref[...] = total.astype(BF16)


def put_both(own_ref, edge_ref, values, has_above, has_below):
    put_bands(own_ref, between(values, BASE, BASE + ROWS, -BASE))
    above = between(values, BASE - 16, BASE, 16 - BASE)
    above = above + between(values, BASE - 17, BASE - 16, 39 - (BASE - 17))
    below = between(values, BASE + ROWS, BASE + ROWS + 18, 16 - BASE - ROWS)
    put_bands(edge_ref, jnp.where(has_above, above, 0.0) + jnp.where(has_below, below, 0.0))


def skewed(ref, lag, rows, shift):
    values = jnp.broadcast_to(ref[lag : lag + 1, :], (rows, SLOT))
    return pltpu.roll(values, shift, 1, stride=1, stride_axis=0)


def bands_kernel(
    place_ref, k1_ref, k2_ref, mix_ref, own1_ref, edge1_ref, own2_ref, above2_ref, below2_ref
):
    has_above, has_below = place_ref[2] > 0, place_ref[2] < 15
    first = jnp.concatenate([skewed(k1_ref, lag, 48, 0) for lag in range(24)], axis=1)
    merged = jnp.dot(
        mix_ref[...], first, precision=lax.Precision.HIGHEST, preferred_element_type=F32
    )
    slots = [merged[:, SLOT * lag : SLOT * (lag + 1)] for lag in range(24)]
    put_both(own1_ref, edge1_ref, jnp.concatenate(slots, axis=0), has_above, has_below)
    slots = [skewed(k2_ref, lag, ROWS, 8) for lag in range(24)]
    values = jnp.concatenate(slots, axis=0)
    put_bands(own2_ref, between(values, BASE, BASE + ROWS, -BASE))
    put_thin_bands(above2_ref, values, BASE - THIN, 0, has_above)
    put_thin_bands(below2_ref, values, BASE + ROWS, ROWS - THIN, has_below)


def coverage(starts, offset, q):
    column = lax.broadcasted_iota(jnp.int32, starts.shape, 1) + q * CHUNK
    actual = column - offset + starts
    return ((actual >= 0) & (actual <= COLS - TAPS)).astype(F32)


def put_blocks(ref, values, row, place_ref, q):
    for j in range(4):
        at = (j % 2) ^ place_ref[1], 2 * q + j // 2, pl.ds(row, ROWS)
        ref[at] = values[:, j * BLOCK : (j + 1) * BLOCK]


def clear(frame_ref, row):
    rows = frame_ref.shape[0]
    frame_ref[:, COLS:FRAME] = jnp.zeros((rows, FRAME - COLS), F32)
    frame_ref[row:rows, 0:COLS] = jnp.zeros((rows - row, COLS), F32)


def put_wide(frame_ref, row, ref, rows):
    for q in range(4):
        cols = pl.ds(q * CHUNK, CHUNK)
        frame_ref[row : row + rows, cols] = ref[rows * q : rows * (q + 1), :]


def put_thin(frame_ref, row, ref, at):
    for q in range(4):
        frame_ref[row : row + 1, q * CHUNK : (q + 1) * CHUNK] = ref[at + q : at + q + 1, :]


def split_rows(frame_ref, halves_ref):
    frame = frame_ref[...]
    padding = jnp.zeros((SLOT - 3 * SPAN, FRAME), F32)
    for part in range(GROUP):
        moved = pltpu.roll(frame, HALF - part, 1)
        high = moved.astype(BF16).astype(F32)
        spans = jnp.concatenate([high, moved - high, high, padding], axis=0)
        halves_ref[SLOT * part : SLOT * (part + 1), :] = spans.astype(BF16)


def correlate_chunk(band_ref, halves_ref, q):
    width = CHUNK + 128
    lags = jnp.dot(
        band_ref[...],
        halves_ref[:, q * CHUNK : q * CHUNK + width],
        preferred_element_type=F32,
    )
    total = lags[0:ROWS, :CHUNK]
    for step in range(1, STEPS):
        moved = pltpu.roll(lags[ROWS * step : ROWS * (step + 1), :], width - GROUP * step, 1)
        total = total + moved[:, :CHUNK]
    return total


def own_and_template_kernel(
    own_ref, band_ref, coadd_ref, out_ref, template_ref, frame_ref, halves_ref
):
    template_ref[...] = coadd_ref[...]
    own_kernel(own_ref, band_ref, out_ref, frame_ref, halves_ref)


def own_kernel(own_ref, band_ref, out_ref, frame_ref, halves_ref):
    clear(frame_ref, ROWS)
    frame_ref[0:ROWS, 0:COLS] = own_ref[...]
    split_rows(frame_ref, halves_ref)
    for q in range(4):
        out_ref[:, q * CHUNK : (q + 1) * CHUNK] = correlate_chunk(band_ref, halves_ref, q)


def warp_kernel(
    place_source_ref,
    weight_source_ref,
    own_ref,
    above_ref,
    below_ref,
    band_ref,
    starts_ref,
    taps_ref,
    mask_ref,
    warped_ref,
    weighted_ref,
    frame_ref,
    halves_ref,
    source_ref,
    place_ref,
    weight_ref,
    sems,
):
    fetches = [
        pltpu.make_async_copy(place_source_ref, place_ref, sems.at[0]),
        pltpu.make_async_copy(weight_source_ref, weight_ref, sems.at[1]),
    ]
    for fetch in fetches:
        fetch.start()
    clear(frame_ref, 32)
    put_wide(frame_ref, 0, above_ref, 16)
    put_wide(frame_ref, 16, below_ref, 16)
    put_thin(frame_ref, 32, below_ref, 64)
    put_thin(frame_ref, 33, below_ref, 68)
    put_thin(frame_ref, 39, above_ref, 64)
    split_rows(frame_ref, halves_ref)

    source_ref[:, 0:LEFT] = jnp.zeros((ROWS, LEFT), F32)
    source_ref[:, LEFT + COLS : LEFT + COLS + 128] = jnp.zeros((ROWS, 128), F32)
    for q in range(4):
        edges = correlate_chunk(band_ref, halves_ref, q)
        source_ref[:, LEFT + q * CHUNK : LEFT + (q + 1) * CHUNK] = (
            own_ref[:, q * CHUNK : (q + 1) * CHUNK] + edges
        )

    for fetch in fetches:
        fetch.wait()
    offset = place_ref[0]
    first = LEFT - 3 - offset
    aligned = first // 128
    rest = first - aligned * 128
    width = CHUNK + 256
    for q in range(4):
        cols = pl.ds(q * CHUNK, CHUNK)
        at = pl.multiple_of((aligned + q * (CHUNK // 128)) * 128, 128)
        moved = pltpu.roll(source_ref[:, pl.ds(at, width)], width - rest, 1)
        starts = starts_ref[:, cols]
        early = starts == -3
        taps = [taps_ref[t : t + 1, cols] for t in range(TAPS)]
        zero = jnp.zeros_like(taps[0])
        total = None
        for lag in range(TAPS + 1):
            tap = jnp.where(
                early, taps[lag] if lag < TAPS else zero, taps[lag - 1] if lag else zero
            )
            part = moved if lag == 0 else pltpu.roll(moved, width - lag, 1)
            term = tap * part[:, :CHUNK]
            total = term if total is None else total + term
        warped_ref[:, cols] = total
        share = weight_ref[0] * mask_ref[:, cols].astype(F32) * coverage(starts, offset, q)
        put_blocks(weighted_ref, share * total, 0, place_ref, q)
        put_blocks(weighted_ref, share, ROWS, place_ref, q)


def differ_kernel(
    first_core_ref,
    own_ref,
    mine_ref,
    other_ref,
    diff_ref,
    up_ref,
    down_ref,
):
    first_core = jnp.broadcast_to(first_core_ref[...], (ROWS, BLOCK)) > 0
    for b in range(16):
        cols = pl.ds(b * BLOCK, BLOCK)
        even, odd = (mine_ref, other_ref) if b % 2 == 0 else (other_ref, mine_ref)
        coadd = jnp.where(first_core, even[b // 2], odd[b // 2])
        diff_ref[:, cols] = own_ref[:, cols] - coadd
    for q in range(4):
        cols = pl.ds(q * CHUNK, CHUNK)
        down_ref[8 * q : 8 * q + 8, :] = diff_ref[24:32, cols]
        up_ref[8 * q : 8 * q + 8, :] = diff_ref[0:8, cols]
        for extra in range(2):
            at = 32 + 4 * extra + q
            down_ref[at : at + 1, :] = diff_ref[22 + extra : 23 + extra, cols]
            up_ref[at : at + 1, :] = diff_ref[8 + extra : 9 + extra, cols]


def thin_edges(own_ref, row, band_ref, out_ref, frame_ref, halves_ref, done_ref, sems):
    frame = frame_ref[...]
    for part in range(THIN_GROUP):
        moved = pltpu.roll(frame, HALF - part, 1)
        high = moved.astype(BF16).astype(F32)
        spans = jnp.concatenate([high, moved - high, high], axis=0)
        halves_ref[3 * THIN * part : 3 * THIN * (part + 1), :] = spans.astype(BF16)
    used = 3 * THIN * THIN_GROUP
    halves_ref[used:256, :] = jnp.zeros((256 - used, FRAME), BF16)
    width = CHUNK + 128
    copies = []
    for q in range(4):
        cols = pl.ds(q * CHUNK, CHUNK)
        lags = jnp.dot(
            band_ref[...],
            halves_ref[:, q * CHUNK : q * CHUNK + width],
            preferred_element_type=F32,
        )
        total = own_ref[row : row + THIN, cols] + lags[0:THIN, :CHUNK]
        for step in range(1, THIN_STEPS):
            lag = lags[THIN * step : THIN * (step + 1), :]
            total = total + pltpu.roll(lag, width - THIN_GROUP * step, 1)[:, :CHUNK]
        done_ref[:, cols] = total
        copy = pltpu.make_async_copy(
            done_ref.at[:, cols], out_ref.at[pl.ds(row, THIN), cols], sems.at[q]
        )
        copy.start()
        copies.append(copy)
    for copy in copies:
        copy.wait()


def above_kernel(
    own_ref,
    above_ref,
    band_ref,
    out_ref,
    frame_ref,
    halves_ref,
    done_ref,
    sems,
):
    clear(frame_ref, 0)
    put_wide(frame_ref, 8, above_ref, 8)
    for extra in range(2):
        put_thin(frame_ref, 6 + extra, above_ref, 32 + 4 * extra)
    thin_edges(own_ref, 0, band_ref, out_ref, frame_ref, halves_ref, done_ref, sems)


def below_kernel(
    own_ref,
    below_ref,
    band_ref,
    begun_ref,
    out_ref,
    frame_ref,
    halves_ref,
    done_ref,
    sems,
):
    clear(frame_ref, 0)
    put_wide(frame_ref, 0, below_ref, 8)
    for extra in range(2):
        put_thin(frame_ref, 8 + extra, below_ref, 32 + 4 * extra)
    row = ROWS - THIN
    thin_edges(own_ref, row, band_ref, out_ref, frame_ref, halves_ref, done_ref, sems)


def by_lag(kernel):
    return jnp.pad(kernel.T, ((0, 3), (LEAD, SLOT - LEAD - KS)))


def swap(values, step):
    return lax.ppermute(values, "visit", [(i, i ^ step) for i in range(16)])


def over_chips(blocks):
    return lax.all_to_all(
        blocks,
        "visit",
        split_axis=0,
        concat_axis=0,
        axis_index_groups=[list(range(core, 16, 2)) for core in range(2)],
        tiled=True,
    )


def to_next(values):
    return lax.ppermute(values, "row", [(i, (i + 1) % 16) for i in range(16)])


def to_previous(values):
    return lax.ppermute(values, "row", [((i + 1) % 16, i) for i in range(16)])


def on_device(
    science,
    basis_kernels,
    basis_coeffs,
    row_starts,
    row_taps,
    col_offsets,
    col_starts,
    col_taps,
    visit_weights,
    clip_masks,
    decorrelation,
):
    pixels = science[0]
    visit = lax.axis_index("visit")
    band = lax.axis_index("row")
    band_at = band * ROWS
    place = jnp.stack([col_offsets[0], visit % 2, band]).astype(jnp.int32)

    above = to_next(call(down_kernel, sds(72, CHUNK), [VM])(pixels))
    below = to_previous(call(up_kernel, sds(72, CHUNK), [VM])(pixels))

    first_core = jnp.full((1, BLOCK), visit % 2 == 0).astype(jnp.int32)
    kernel = jnp.einsum(
        "b,bij->ij", basis_coeffs[0], basis_kernels, precision=lax.Precision.HIGHEST
    )
    matched_row = jnp.arange(48, dtype=jnp.int32)[None, :] - 8
    tap_at = matched_row - (jnp.arange(ROWS, dtype=jnp.int32) + row_starts[0])[:, None]
    inside = (matched_row + band_at >= 0) & (matched_row + band_at < 16 * ROWS)
    hits = tap_at[None] == jnp.arange(TAPS, dtype=jnp.int32)[:, None, None]
    mix = jnp.sum(jnp.where(hits & inside[None], row_taps[0][:, :, None], 0.0), axis=0)
    bands = sds(STEPS * ROWS, GROUP * SLOT, dtype=BF16)
    thin_bands = sds(THIN_STEPS * THIN, 256, dtype=BF16)
    own_first, edge_first, own_second, above_second, below_second = call(
        bands_kernel, (bands, bands, bands, thin_bands, thin_bands), [SM] + [VM] * 3
    )(place, by_lag(kernel), by_lag(decorrelation[0]), mix)

    frames = [
        pltpu.VMEM((SPAN, FRAME), F32),
        pltpu.VMEM((GROUP * SLOT, FRAME), BF16),
    ]
    own_part = call(own_kernel, sds(ROWS, COLS), [VM] * 2, frames)(pixels, own_first)
    warped, weighted = call(
        warp_kernel,
        (sds(ROWS, COLS), sds(2, 8, 2 * ROWS, BLOCK)),
        [ANY, ANY] + [VM] * 7,
        frames
        + [
            pltpu.VMEM((ROWS, LEFT + COLS + 128), F32),
            pltpu.SMEM((3,), jnp.int32),
            pltpu.SMEM((1,), F32),
            pltpu.SemaphoreType.DMA((2,)),
        ],
    )(
        place,
        visit_weights,
        own_part,
        above,
        below,
        edge_first,
        col_starts,
        col_taps[0],
        clip_masks[0],
    )
    half = weighted[0] + swap(weighted[1], 1)
    total = jnp.sum(over_chips(half), axis=0)
    coadd = total[:ROWS] / jnp.maximum(total[ROWS:], 1.0)
    mine = over_chips(jnp.broadcast_to(coadd[None], (8, ROWS, BLOCK)))
    other = swap(mine, 1)
    difference, up, down = call(
        differ_kernel,
        (sds(ROWS, COLS), sds(40, CHUNK), sds(40, CHUNK)),
        [VM] * 4,
    )(first_core, warped, mine, other)
    above, below = to_next(down), to_previous(up)
    own_part, template = call(
        own_and_template_kernel, (sds(ROWS, COLS), sds(ROWS, BLOCK)), [VM] * 3, frames
    )(difference, own_second, coadd)
    thin_frames = [
        pltpu.VMEM((THIN, FRAME), F32),
        pltpu.VMEM((256, FRAME), BF16),
        pltpu.VMEM((THIN, COLS), F32),
        pltpu.SemaphoreType.DMA((4,)),
    ]
    begun = call(above_kernel, sds(ROWS, COLS), [VM] * 3, thin_frames, ANY)(
        own_part, above, above_second
    )
    cleaned = call(
        below_kernel, sds(ROWS, COLS), [VM] * 3 + [ANY], thin_frames, ANY, {3: 0}
    )(own_part, below, below_second, begun)
    return cleaned[None], template


def solution(mesh):
    return jax.shard_map(
        on_device,
        mesh=mesh,
        in_specs=(
            P("visit", "row", None),
            P(),
            P("visit", None),
            P("visit", "row"),
            P("visit", None, "row"),
            P("visit"),
            P("visit", None),
            P("visit", None, None),
            P("visit"),
            P("visit", "row", None),
            P("visit", None, None),
        ),
        out_specs=(P("visit", "row", None), P("row", "visit")),
        check_vma=False,
    )
```

```python
import jax
import jax.numpy as jnp
from jax import lax
from jax.experimental import pallas as pl
from jax.experimental.pallas import tpu as pltpu
from jax.sharding import PartitionSpec as P

KS = 21
HALF = KS // 2
TAPS = 8
ROWS = 32
COLS = 4096
SPAN = 40
SLOT = 128
BASE = 24
LEAD = 6
CHUNK = 1024
BLOCK = 256
GROUP = 4
STEPS = 6
THIN = 16
THIN_GROUP = 5
THIN_STEPS = 5
FRAME = COLS + 128
LEFT = 640
F32 = jnp.float32
BF16 = jnp.bfloat16
VMEM_LIMIT = 16 * 1024 * 1024

VM = pl.BlockSpec(memory_space=pltpu.VMEM)
SM = pl.BlockSpec(memory_space=pltpu.SMEM)


ANY = pl.BlockSpec(memory_space=pl.ANY)


def call(kernel, outs, ins, scratch=(), places=None, aliases=None):
    return pl.pallas_call(
        kernel,
        out_shape=outs,
        in_specs=ins,
        out_specs=jax.tree.map(lambda _: VM, outs) if places is None else places,
        scratch_shapes=list(scratch),
        input_output_aliases=aliases or {},
        compiler_params=pltpu.CompilerParams(vmem_limit_bytes=VMEM_LIMIT),
    )


def sds(*shape, dtype=F32):
    return jax.ShapeDtypeStruct(shape, dtype)


def down_kernel(x_ref, down_ref):
    for q in range(4):
        cols = pl.ds(q * CHUNK, CHUNK)
        down_ref[16 * q : 16 * q + 16, :] = x_ref[16:32, cols]
        down_ref[64 + q : 65 + q, :] = x_ref[15:16, cols]
        down_ref[68 + q : 69 + q, :] = jnp.zeros((1, CHUNK), F32)


def up_kernel(x_ref, up_ref):
    for q in range(4):
        cols = pl.ds(q * CHUNK, CHUNK)
        up_ref[16 * q : 16 * q + 16, :] = x_ref[0:16, cols]
        up_ref[64 + q : 65 + q, :] = x_ref[16:17, cols]
        up_ref[68 + q : 69 + q, :] = x_ref[17:18, cols]


def between(values, low, high, shift):
    lanes = lax.broadcasted_iota(jnp.int32, values.shape, 1)
    return pltpu.roll(jnp.where((lanes >= low) & (lanes < high), values, 0.0), shift % SLOT, 1)


def put_bands(ref, values):
    lanes = lax.broadcasted_iota(jnp.int32, values.shape, 1)
    spans = values + pltpu.roll(values, SPAN, 1) + pltpu.roll(values, 2 * SPAN, 1)
    high = spans.astype(BF16).astype(F32)
    parts = jnp.where(lanes < 2 * SPAN, high, spans - high).astype(BF16)
    for lag in range(GROUP * STEPS):
        rows = pl.ds(ROWS * (lag // GROUP), ROWS)
        slot = pl.ds(SLOT * (lag % GROUP), SLOT)
        ref[rows, slot] = parts[ROWS * lag : ROWS * (lag + 1)]


def put_thin_bands(ref, values, low, row, valid):
    lanes = lax.broadcasted_iota(jnp.int32, values.shape, 1)
    span = jnp.where(valid, between(values, low, low + THIN, -low), 0.0)
    spans = span + pltpu.roll(span, THIN, 1) + pltpu.roll(span, 2 * THIN, 1)
    high = spans.astype(BF16).astype(F32)
    parts = jnp.where(lanes < 2 * THIN, high, spans - high)
    total = None
    for part in range(THIN_GROUP):
        rows = []
        for step in range(THIN_STEPS):
            at = ROWS * (THIN_GROUP * step + part) + row
            known = at < values.shape[0]
            rows.append(parts[at : at + THIN] if known else jnp.zeros((THIN, SLOT), F32))
        stacked = jnp.concatenate(rows, axis=0)
        wide = jnp.concatenate([stacked, jnp.zeros_like(stacked)], axis=1)
        moved = pltpu.roll(wide, 3 * THIN * part, 1) if part else wide
        total = moved if total is None else total + moved
    ref[...] = total.astype(BF16)


def put_both(own_ref, edge_ref, values, has_above, has_below):
    put_bands(own_ref, between(values, BASE, BASE + ROWS, -BASE))
    above = between(values, BASE - 16, BASE, 16 - BASE)
    above = above + between(values, BASE - 17, BASE - 16, 39 - (BASE - 17))
    below = between(values, BASE + ROWS, BASE + ROWS + 18, 16 - BASE - ROWS)
    put_bands(edge_ref, jnp.where(has_above, above, 0.0) + jnp.where(has_below, below, 0.0))


def skewed(ref, lag, rows, shift):
    values = jnp.broadcast_to(ref[lag : lag + 1, :], (rows, SLOT))
    return pltpu.roll(values, shift, 1, stride=1, stride_axis=0)


def first_bands_kernel(place_ref, lags_ref, mix_ref, own_ref, edge_ref):
    has_above, has_below = place_ref[2] > 0, place_ref[2] < 15
    values = jnp.concatenate([skewed(lags_ref, lag, 48, 0) for lag in range(24)], axis=1)
    merged = jnp.dot(
        mix_ref[...], values, precision=lax.Precision.HIGHEST, preferred_element_type=F32
    )
    slots = [merged[:, SLOT * lag : SLOT * (lag + 1)] for lag in range(24)]
    put_both(own_ref, edge_ref, jnp.concatenate(slots, axis=0), has_above, has_below)


def second_bands_kernel(place_ref, lags_ref, own_ref, above_ref, below_ref):
    slots = [skewed(lags_ref, lag, ROWS, 8) for lag in range(24)]
    values = jnp.concatenate(slots, axis=0)
    put_bands(own_ref, between(values, BASE, BASE + ROWS, -BASE))
    put_thin_bands(above_ref, values, BASE - THIN, 0, place_ref[2] > 0)
    put_thin_bands(below_ref, values, BASE + ROWS, ROWS - THIN, place_ref[2] < 15)


def coverage(starts, offset, q):
    column = lax.broadcasted_iota(jnp.int32, starts.shape, 1) + q * CHUNK
    actual = column - offset + starts
    return ((actual >= 0) & (actual <= COLS - TAPS)).astype(F32)


def put_blocks(kept_ref, sent_ref, values, core, q):
    blocks = [values[:, j * BLOCK : (j + 1) * BLOCK] for j in range(4)]
    for j in range(2):
        even, odd = blocks[2 * j : 2 * j + 2]
        kept_ref[2 * q + j] = jnp.where(core == 0, even, odd)
        sent_ref[2 * q + j] = jnp.where(core == 0, odd, even)


def share_kernel(place_ref, weight_ref, mask_ref, starts_ref, kept_ref, sent_ref):
    for q in range(4):
        cols = pl.ds(q * CHUNK, CHUNK)
        covered = coverage(starts_ref[:, cols], place_ref[0], q)
        share = weight_ref[0] * mask_ref[:, cols].astype(F32) * covered
        put_blocks(kept_ref, sent_ref, share, place_ref[1], q)


def clear(frame_ref, row):
    rows = frame_ref.shape[0]
    frame_ref[:, COLS:FRAME] = jnp.zeros((rows, FRAME - COLS), F32)
    frame_ref[row:rows, 0:COLS] = jnp.zeros((rows - row, COLS), F32)


def put_wide(frame_ref, row, ref, rows):
    for q in range(4):
        cols = pl.ds(q * CHUNK, CHUNK)
        frame_ref[row : row + rows, cols] = ref[rows * q : rows * (q + 1), :]


def put_thin(frame_ref, row, ref, at):
    for q in range(4):
        frame_ref[row : row + 1, q * CHUNK : (q + 1) * CHUNK] = ref[at + q : at + q + 1, :]


def split_rows(frame_ref, halves_ref):
    frame = frame_ref[...]
    padding = jnp.zeros((SLOT - 3 * SPAN, FRAME), F32)
    for part in range(GROUP):
        moved = pltpu.roll(frame, HALF - part, 1)
        high = moved.astype(BF16).astype(F32)
        spans = jnp.concatenate([high, moved - high, high, padding], axis=0)
        halves_ref[SLOT * part : SLOT * (part + 1), :] = spans.astype(BF16)


def correlate_chunk(band_ref, halves_ref, q):
    width = CHUNK + 128
    lags = jnp.dot(
        band_ref[...],
        halves_ref[:, q * CHUNK : q * CHUNK + width],
        preferred_element_type=F32,
    )
    total = lags[0:ROWS, :CHUNK]
    for step in range(1, STEPS):
        moved = pltpu.roll(lags[ROWS * step : ROWS * (step + 1), :], width - GROUP * step, 1)
        total = total + moved[:, :CHUNK]
    return total


def own_and_template_kernel(
    own_ref, band_ref, coadd_ref, out_ref, template_ref, frame_ref, halves_ref
):
    template_ref[...] = coadd_ref[...]
    own_kernel(own_ref, band_ref, out_ref, frame_ref, halves_ref)


def own_kernel(own_ref, band_ref, out_ref, frame_ref, halves_ref):
    clear(frame_ref, ROWS)
    frame_ref[0:ROWS, 0:COLS] = own_ref[...]
    split_rows(frame_ref, halves_ref)
    for q in range(4):
        out_ref[:, q * CHUNK : (q + 1) * CHUNK] = correlate_chunk(band_ref, halves_ref, q)


def warp_kernel(
    place_source_ref,
    weight_source_ref,
    own_ref,
    above_ref,
    below_ref,
    band_ref,
    starts_ref,
    taps_ref,
    mask_ref,
    warped_ref,
    kept_ref,
    sent_ref,
    frame_ref,
    halves_ref,
    source_ref,
    place_ref,
    weight_ref,
    sems,
):
    fetches = [
        pltpu.make_async_copy(place_source_ref, place_ref, sems.at[0]),
        pltpu.make_async_copy(weight_source_ref, weight_ref, sems.at[1]),
    ]
    for fetch in fetches:
        fetch.start()
    clear(frame_ref, 32)
    put_wide(frame_ref, 0, above_ref, 16)
    put_wide(frame_ref, 16, below_ref, 16)
    put_thin(frame_ref, 32, below_ref, 64)
    put_thin(frame_ref, 33, below_ref, 68)
    put_thin(frame_ref, 39, above_ref, 64)
    split_rows(frame_ref, halves_ref)

    source_ref[:, 0:LEFT] = jnp.zeros((ROWS, LEFT), F32)
    source_ref[:, LEFT + COLS : LEFT + COLS + 128] = jnp.zeros((ROWS, 128), F32)
    for q in range(4):
        edges = correlate_chunk(band_ref, halves_ref, q)
        source_ref[:, LEFT + q * CHUNK : LEFT + (q + 1) * CHUNK] = (
            own_ref[:, q * CHUNK : (q + 1) * CHUNK] + edges
        )

    for fetch in fetches:
        fetch.wait()
    offset = place_ref[0]
    first = LEFT - 3 - offset
    aligned = first // 128
    rest = first - aligned * 128
    width = CHUNK + 256
    for q in range(4):
        cols = pl.ds(q * CHUNK, CHUNK)
        at = pl.multiple_of((aligned + q * (CHUNK // 128)) * 128, 128)
        moved = pltpu.roll(source_ref[:, pl.ds(at, width)], width - rest, 1)
        moved = moved[:, : CHUNK + 128]
        starts = starts_ref[:, cols]
        early = starts == -3
        taps = [taps_ref[t : t + 1, cols] for t in range(TAPS)]
        zero = jnp.zeros_like(taps[0])
        total = None
        for lag in range(TAPS + 1):
            tap = jnp.where(
                early, taps[lag] if lag < TAPS else zero, taps[lag - 1] if lag else zero
            )
            part = moved if lag == 0 else pltpu.roll(moved, CHUNK + 128 - lag, 1)
            term = tap * part[:, :CHUNK]
            total = term if total is None else total + term
        warped_ref[:, cols] = total
        share = weight_ref[0] * mask_ref[:, cols].astype(F32) * coverage(starts, offset, q)
        put_blocks(kept_ref, sent_ref, share * total, place_ref[1], q)


def differ_kernel(
    first_core_ref,
    own_ref,
    mine_ref,
    other_ref,
    diff_ref,
    up_ref,
    down_ref,
):
    first_core = jnp.broadcast_to(first_core_ref[...], (ROWS, BLOCK)) > 0
    for b in range(16):
        cols = pl.ds(b * BLOCK, BLOCK)
        even, odd = (mine_ref, other_ref) if b % 2 == 0 else (other_ref, mine_ref)
        coadd = jnp.where(first_core, even[b // 2], odd[b // 2])
        diff_ref[:, cols] = own_ref[:, cols] - coadd
    for q in range(4):
        cols = pl.ds(q * CHUNK, CHUNK)
        down_ref[8 * q : 8 * q + 8, :] = diff_ref[24:32, cols]
        up_ref[8 * q : 8 * q + 8, :] = diff_ref[0:8, cols]
        for extra in range(2):
            at = 32 + 4 * extra + q
            down_ref[at : at + 1, :] = diff_ref[22 + extra : 23 + extra, cols]
            up_ref[at : at + 1, :] = diff_ref[8 + extra : 9 + extra, cols]


def thin_edges(own_ref, row, band_ref, out_ref, frame_ref, halves_ref, done_ref, sems):
    frame = frame_ref[...]
    for part in range(THIN_GROUP):
        moved = pltpu.roll(frame, HALF - part, 1)
        high = moved.astype(BF16).astype(F32)
        spans = jnp.concatenate([high, moved - high, high], axis=0)
        halves_ref[3 * THIN * part : 3 * THIN * (part + 1), :] = spans.astype(BF16)
    used = 3 * THIN * THIN_GROUP
    halves_ref[used:256, :] = jnp.zeros((256 - used, FRAME), BF16)
    width = CHUNK + 128
    copies = []
    for q in range(4):
        cols = pl.ds(q * CHUNK, CHUNK)
        lags = jnp.dot(
            band_ref[...],
            halves_ref[:, q * CHUNK : q * CHUNK + width],
            preferred_element_type=F32,
        )
        total = own_ref[row : row + THIN, cols] + lags[0:THIN, :CHUNK]
        for step in range(1, THIN_STEPS):
            lag = lags[THIN * step : THIN * (step + 1), :]
            total = total + pltpu.roll(lag, width - THIN_GROUP * step, 1)[:, :CHUNK]
        done_ref[:, cols] = total
        copy = pltpu.make_async_copy(
            done_ref.at[:, cols], out_ref.at[pl.ds(row, THIN), cols], sems.at[q]
        )
        copy.start()
        copies.append(copy)
    for copy in copies:
        copy.wait()


def above_kernel(
    own_ref,
    above_ref,
    band_ref,
    out_ref,
    frame_ref,
    halves_ref,
    done_ref,
    sems,
):
    clear(frame_ref, 0)
    put_wide(frame_ref, 8, above_ref, 8)
    for extra in range(2):
        put_thin(frame_ref, 6 + extra, above_ref, 32 + 4 * extra)
    thin_edges(own_ref, 0, band_ref, out_ref, frame_ref, halves_ref, done_ref, sems)


def below_kernel(
    own_ref,
    below_ref,
    band_ref,
    begun_ref,
    out_ref,
    frame_ref,
    halves_ref,
    done_ref,
    sems,
):
    clear(frame_ref, 0)
    put_wide(frame_ref, 0, below_ref, 8)
    for extra in range(2):
        put_thin(frame_ref, 8 + extra, below_ref, 32 + 4 * extra)
    row = ROWS - THIN
    thin_edges(own_ref, row, band_ref, out_ref, frame_ref, halves_ref, done_ref, sems)


def by_lag(kernel):
    return jnp.pad(kernel.T, ((0, 3), (LEAD, SLOT - LEAD - KS)))


def swap(values, step):
    return lax.ppermute(values, "visit", [(i, i ^ step) for i in range(16)])


def over_chips(blocks):
    return lax.all_to_all(
        blocks,
        "visit",
        split_axis=0,
        concat_axis=0,
        axis_index_groups=[list(range(core, 16, 2)) for core in range(2)],
        tiled=True,
    )


def to_next(values):
    return lax.ppermute(values, "row", [(i, (i + 1) % 16) for i in range(16)])


def to_previous(values):
    return lax.ppermute(values, "row", [((i + 1) % 16, i) for i in range(16)])


def on_device(
    science,
    basis_kernels,
    basis_coeffs,
    row_starts,
    row_taps,
    col_offsets,
    col_starts,
    col_taps,
    visit_weights,
    clip_masks,
    decorrelation,
):
    pixels = science[0]
    visit = lax.axis_index("visit")
    band = lax.axis_index("row")
    band_at = band * ROWS
    place = jnp.stack([col_offsets[0], visit % 2, band]).astype(jnp.int32)

    above = to_next(call(down_kernel, sds(72, CHUNK), [VM])(pixels))
    below = to_previous(call(up_kernel, sds(72, CHUNK), [VM])(pixels))

    first_core = jnp.full((1, BLOCK), visit % 2 == 0).astype(jnp.int32)
    kernel = jnp.einsum(
        "b,bij->ij", basis_coeffs[0], basis_kernels, precision=lax.Precision.HIGHEST
    )
    matched_row = jnp.arange(48, dtype=jnp.int32)[None, :] - 8
    tap_at = matched_row - (jnp.arange(ROWS, dtype=jnp.int32) + row_starts[0])[:, None]
    inside = (matched_row + band_at >= 0) & (matched_row + band_at < 16 * ROWS)
    hits = tap_at[None] == jnp.arange(TAPS, dtype=jnp.int32)[:, None, None]
    mix = jnp.sum(jnp.where(hits & inside[None], row_taps[0][:, :, None], 0.0), axis=0)
    bands = sds(STEPS * ROWS, GROUP * SLOT, dtype=BF16)
    thin_bands = sds(THIN_STEPS * THIN, 256, dtype=BF16)
    own_first, edge_first = call(first_bands_kernel, (bands, bands), [SM] + [VM] * 2)(
        place, by_lag(kernel), mix
    )

    frames = [
        pltpu.VMEM((SPAN, FRAME), F32),
        pltpu.VMEM((GROUP * SLOT, FRAME), BF16),
    ]
    own_part = call(own_kernel, sds(ROWS, COLS), [VM] * 2, frames)(pixels, own_first)
    blocks = sds(8, ROWS, BLOCK)
    kept, sent = call(share_kernel, (blocks, blocks), [SM, SM, VM, VM])(
        place, visit_weights, clip_masks[0], col_starts
    )
    shares = kept + swap(sent, 1)
    denominator = jnp.maximum(jnp.sum(over_chips(shares), axis=0), 1.0)
    warped, kept, sent = call(
        warp_kernel,
        (sds(ROWS, COLS), blocks, blocks),
        [ANY, ANY] + [VM] * 7,
        frames
        + [
            pltpu.VMEM((ROWS, LEFT + COLS + 128), F32),
            pltpu.SMEM((3,), jnp.int32),
            pltpu.SMEM((1,), F32),
            pltpu.SemaphoreType.DMA((2,)),
        ],
    )(
        place,
        visit_weights,
        own_part,
        above,
        below,
        edge_first,
        col_starts,
        col_taps[0],
        clip_masks[0],
    )
    sent, denominator = lax.optimization_barrier((sent, denominator))
    second_lags, kept = lax.optimization_barrier((by_lag(decorrelation[0]), kept))
    own_second, above_second, below_second = call(
        second_bands_kernel, (bands, thin_bands, thin_bands), [SM, VM]
    )(place, second_lags)
    half = kept + swap(sent, 1)
    half, own_second = lax.optimization_barrier((half, own_second))
    coadd = jnp.sum(over_chips(half), axis=0) / denominator
    mine = over_chips(jnp.broadcast_to(coadd[None], (8, ROWS, BLOCK)))
    other = swap(mine, 1)
    difference, up, down = call(
        differ_kernel,
        (sds(ROWS, COLS), sds(40, CHUNK), sds(40, CHUNK)),
        [VM] * 4,
    )(first_core, warped, mine, other)
    above, below = to_next(down), to_previous(up)
    own_part, template = call(
        own_and_template_kernel, (sds(ROWS, COLS), sds(ROWS, BLOCK)), [VM] * 3, frames
    )(difference, own_second, coadd)
    thin_frames = [
        pltpu.VMEM((THIN, FRAME), F32),
        pltpu.VMEM((256, FRAME), BF16),
        pltpu.VMEM((THIN, COLS), F32),
        pltpu.SemaphoreType.DMA((4,)),
    ]
    begun = call(above_kernel, sds(ROWS, COLS), [VM] * 3, thin_frames, ANY)(
        own_part, above, above_second
    )
    cleaned = call(
        below_kernel, sds(ROWS, COLS), [VM] * 3 + [ANY], thin_frames, ANY, {3: 0}
    )(own_part, below, below_second, begun)
    return cleaned[None], template


def solution(mesh):
    return jax.shard_map(
        on_device,
        mesh=mesh,
        in_specs=(
            P("visit", "row", None),
            P(),
            P("visit", None),
            P("visit", "row"),
            P("visit", None, "row"),
            P("visit"),
            P("visit", None),
            P("visit", None, None),
            P("visit"),
            P("visit", "row", None),
            P("visit", None, None),
        ),
        out_specs=(P("visit", "row", None), P("row", "visit")),
        check_vma=False,
    )
```

```python
import jax
import jax.numpy as jnp
from jax import lax
from jax.experimental import pallas as pl
from jax.experimental.pallas import tpu as pltpu
from jax.sharding import PartitionSpec as P

KS = 21
HALF = KS // 2
TAPS = 8
ROWS = 32
COLS = 4096
SPAN = 40
SLOT = 128
BASE = 24
LEAD = 6
CHUNK = 1024
BLOCK = 256
GROUP = 4
STEPS = 6
THIN = 16
THIN_GROUP = 5
THIN_STEPS = 5
FRAME = COLS + 128
LEFT = 640
F32 = jnp.float32
BF16 = jnp.bfloat16
VMEM_LIMIT = 16 * 1024 * 1024

VM = pl.BlockSpec(memory_space=pltpu.VMEM)
SM = pl.BlockSpec(memory_space=pltpu.SMEM)


ANY = pl.BlockSpec(memory_space=pl.ANY)


def call(kernel, outs, ins, scratch=(), places=None, aliases=None):
    return pl.pallas_call(
        kernel,
        out_shape=outs,
        in_specs=ins,
        out_specs=jax.tree.map(lambda _: VM, outs) if places is None else places,
        scratch_shapes=list(scratch),
        input_output_aliases=aliases or {},
        compiler_params=pltpu.CompilerParams(vmem_limit_bytes=VMEM_LIMIT),
    )


def sds(*shape, dtype=F32):
    return jax.ShapeDtypeStruct(shape, dtype)


def down_kernel(x_ref, down_ref):
    for q in range(4):
        cols = pl.ds(q * CHUNK, CHUNK)
        down_ref[16 * q : 16 * q + 16, :] = x_ref[16:32, cols]
        down_ref[64 + q : 65 + q, :] = x_ref[15:16, cols]
        down_ref[68 + q : 69 + q, :] = jnp.zeros((1, CHUNK), F32)


def up_kernel(x_ref, up_ref):
    for q in range(4):
        cols = pl.ds(q * CHUNK, CHUNK)
        up_ref[16 * q : 16 * q + 16, :] = x_ref[0:16, cols]
        up_ref[64 + q : 65 + q, :] = x_ref[16:17, cols]
        up_ref[68 + q : 69 + q, :] = x_ref[17:18, cols]


def between(values, low, high, shift):
    lanes = lax.broadcasted_iota(jnp.int32, values.shape, 1)
    return pltpu.roll(jnp.where((lanes >= low) & (lanes < high), values, 0.0), shift % SLOT, 1)


def put_bands(ref, values):
    lanes = lax.broadcasted_iota(jnp.int32, values.shape, 1)
    spans = values + pltpu.roll(values, SPAN, 1) + pltpu.roll(values, 2 * SPAN, 1)
    high = spans.astype(BF16).astype(F32)
    parts = jnp.where(lanes < 2 * SPAN, high, spans - high).astype(BF16)
    for lag in range(GROUP * STEPS):
        rows = pl.ds(ROWS * (lag // GROUP), ROWS)
        slot = pl.ds(SLOT * (lag % GROUP), SLOT)
        ref[rows, slot] = parts[ROWS * lag : ROWS * (lag + 1)]


def put_thin_bands(ref, values, low, row, valid):
    lanes = lax.broadcasted_iota(jnp.int32, values.shape, 1)
    span = jnp.where(valid, between(values, low, low + THIN, -low), 0.0)
    spans = span + pltpu.roll(span, THIN, 1) + pltpu.roll(span, 2 * THIN, 1)
    high = spans.astype(BF16).astype(F32)
    parts = jnp.where(lanes < 2 * THIN, high, spans - high)
    total = None
    for part in range(THIN_GROUP):
        rows = []
        for step in range(THIN_STEPS):
            at = ROWS * (THIN_GROUP * step + part) + row
            known = at < values.shape[0]
            rows.append(parts[at : at + THIN] if known else jnp.zeros((THIN, SLOT), F32))
        stacked = jnp.concatenate(rows, axis=0)
        wide = jnp.concatenate([stacked, jnp.zeros_like(stacked)], axis=1)
        moved = pltpu.roll(wide, 3 * THIN * part, 1) if part else wide
        total = moved if total is None else total + moved
    ref[...] = total.astype(BF16)


def put_both(own_ref, edge_ref, values, has_above, has_below):
    put_bands(own_ref, between(values, BASE, BASE + ROWS, -BASE))
    above = between(values, BASE - 16, BASE, 16 - BASE)
    above = above + between(values, BASE - 17, BASE - 16, 39 - (BASE - 17))
    below = between(values, BASE + ROWS, BASE + ROWS + 18, 16 - BASE - ROWS)
    put_bands(edge_ref, jnp.where(has_above, above, 0.0) + jnp.where(has_below, below, 0.0))


def skewed(ref, lag, rows, shift):
    values = jnp.broadcast_to(ref[lag : lag + 1, :], (rows, SLOT))
    return pltpu.roll(values, shift, 1, stride=1, stride_axis=0)


def first_bands_kernel(valid_ref, lags_ref, mix_ref, own_ref, edge_ref):
    shape = (ROWS * GROUP * STEPS, SLOT)
    has_above = jnp.broadcast_to(valid_ref[0:1, :], shape) > 0
    has_below = jnp.broadcast_to(valid_ref[1:2, :], shape) > 0
    values = jnp.concatenate([skewed(lags_ref, lag, 48, 0) for lag in range(24)], axis=1)
    merged = jnp.dot(
        mix_ref[...], values, precision=lax.Precision.HIGHEST, preferred_element_type=F32
    )
    slots = [merged[:, SLOT * lag : SLOT * (lag + 1)] for lag in range(24)]
    put_both(own_ref, edge_ref, jnp.concatenate(slots, axis=0), has_above, has_below)


def second_bands_kernel(valid_ref, lags_ref, own_ref, above_ref, below_ref):
    slots = [skewed(lags_ref, lag, ROWS, 8) for lag in range(24)]
    values = jnp.concatenate(slots, axis=0)
    put_bands(own_ref, between(values, BASE, BASE + ROWS, -BASE))
    has_above = jnp.broadcast_to(valid_ref[0:1, :], values.shape) > 0
    has_below = jnp.broadcast_to(valid_ref[1:2, :], values.shape) > 0
    put_thin_bands(above_ref, values, BASE - THIN, 0, has_above)
    put_thin_bands(below_ref, values, BASE + ROWS, ROWS - THIN, has_below)


def coverage(starts, offset, q):
    column = lax.broadcasted_iota(jnp.int32, starts.shape, 1) + q * CHUNK
    actual = column - offset + starts
    return ((actual >= 0) & (actual <= COLS - TAPS)).astype(F32)


def put_blocks(kept_ref, sent_ref, values, core, q):
    blocks = [values[:, j * BLOCK : (j + 1) * BLOCK] for j in range(4)]
    for j in range(2):
        even, odd = blocks[2 * j : 2 * j + 2]
        kept_ref[2 * q + j] = jnp.where(core == 0, even, odd)
        sent_ref[2 * q + j] = jnp.where(core == 0, odd, even)


def share_kernel(place_ref, weight_ref, mask_ref, starts_ref, kept_ref, sent_ref):
    for q in range(4):
        cols = pl.ds(q * CHUNK, CHUNK)
        covered = coverage(starts_ref[:, cols], place_ref[0], q)
        share = weight_ref[0] * mask_ref[:, cols].astype(F32) * covered
        put_blocks(kept_ref, sent_ref, share, place_ref[1], q)


def clear(frame_ref, row):
    rows = frame_ref.shape[0]
    frame_ref[:, COLS:FRAME] = jnp.zeros((rows, FRAME - COLS), F32)
    frame_ref[row:rows, 0:COLS] = jnp.zeros((rows - row, COLS), F32)


def put_wide(frame_ref, row, ref, rows):
    for q in range(4):
        cols = pl.ds(q * CHUNK, CHUNK)
        frame_ref[row : row + rows, cols] = ref[rows * q : rows * (q + 1), :]


def put_thin(frame_ref, row, ref, at):
    for q in range(4):
        frame_ref[row : row + 1, q * CHUNK : (q + 1) * CHUNK] = ref[at + q : at + q + 1, :]


def split_rows(frame_ref, halves_ref):
    frame = frame_ref[...]
    padding = jnp.zeros((SLOT - 3 * SPAN, FRAME), F32)
    for part in range(GROUP):
        moved = pltpu.roll(frame, HALF - part, 1)
        high = moved.astype(BF16).astype(F32)
        spans = jnp.concatenate([high, moved - high, high, padding], axis=0)
        halves_ref[SLOT * part : SLOT * (part + 1), :] = spans.astype(BF16)


def correlate_chunk(band_ref, halves_ref, q):
    width = CHUNK + 128
    lags = jnp.dot(
        band_ref[...],
        halves_ref[:, q * CHUNK : q * CHUNK + width],
        preferred_element_type=F32,
    )
    total = lags[0:ROWS, :CHUNK]
    for step in range(1, STEPS):
        moved = pltpu.roll(lags[ROWS * step : ROWS * (step + 1), :], width - GROUP * step, 1)
        total = total + moved[:, :CHUNK]
    return total


def own_and_template_kernel(
    own_ref, band_ref, coadd_ref, out_ref, template_ref, frame_ref, halves_ref
):
    template_ref[...] = coadd_ref[...]
    own_kernel(own_ref, band_ref, out_ref, frame_ref, halves_ref)


def own_kernel(own_ref, band_ref, out_ref, frame_ref, halves_ref):
    clear(frame_ref, ROWS)
    frame_ref[0:ROWS, 0:COLS] = own_ref[...]
    split_rows(frame_ref, halves_ref)
    for q in range(4):
        out_ref[:, q * CHUNK : (q + 1) * CHUNK] = correlate_chunk(band_ref, halves_ref, q)


def warp_kernel(
    place_source_ref,
    weight_source_ref,
    own_ref,
    above_ref,
    below_ref,
    band_ref,
    starts_ref,
    taps_ref,
    mask_ref,
    warped_ref,
    kept_ref,
    sent_ref,
    frame_ref,
    halves_ref,
    source_ref,
    place_ref,
    weight_ref,
    sems,
):
    fetches = [
        pltpu.make_async_copy(place_source_ref, place_ref, sems.at[0]),
        pltpu.make_async_copy(weight_source_ref, weight_ref, sems.at[1]),
    ]
    for fetch in fetches:
        fetch.start()
    clear(frame_ref, 32)
    put_wide(frame_ref, 0, above_ref, 16)
    put_wide(frame_ref, 16, below_ref, 16)
    put_thin(frame_ref, 32, below_ref, 64)
    put_thin(frame_ref, 33, below_ref, 68)
    put_thin(frame_ref, 39, above_ref, 64)
    split_rows(frame_ref, halves_ref)

    source_ref[:, 0:LEFT] = jnp.zeros((ROWS, LEFT), F32)
    source_ref[:, LEFT + COLS : LEFT + COLS + 128] = jnp.zeros((ROWS, 128), F32)
    for q in range(4):
        edges = correlate_chunk(band_ref, halves_ref, q)
        source_ref[:, LEFT + q * CHUNK : LEFT + (q + 1) * CHUNK] = (
            own_ref[:, q * CHUNK : (q + 1) * CHUNK] + edges
        )

    for fetch in fetches:
        fetch.wait()
    offset = place_ref[0]
    first = LEFT - 3 - offset
    aligned = first // 128
    rest = first - aligned * 128
    width = CHUNK + 256
    for q in range(4):
        cols = pl.ds(q * CHUNK, CHUNK)
        at = pl.multiple_of((aligned + q * (CHUNK // 128)) * 128, 128)
        moved = pltpu.roll(source_ref[:, pl.ds(at, width)], width - rest, 1)
        moved = moved[:, : CHUNK + 128]
        starts = starts_ref[:, cols]
        early = starts == -3
        taps = [taps_ref[t : t + 1, cols] for t in range(TAPS)]
        zero = jnp.zeros_like(taps[0])
        total = None
        for lag in range(TAPS + 1):
            tap = jnp.where(
                early, taps[lag] if lag < TAPS else zero, taps[lag - 1] if lag else zero
            )
            part = moved if lag == 0 else pltpu.roll(moved, CHUNK + 128 - lag, 1)
            term = tap * part[:, :CHUNK]
            total = term if total is None else total + term
        warped_ref[:, cols] = total
        share = weight_ref[0] * mask_ref[:, cols].astype(F32) * coverage(starts, offset, q)
        put_blocks(kept_ref, sent_ref, share * total, place_ref[1], q)


def differ_kernel(
    first_core_ref,
    own_ref,
    mine_ref,
    other_ref,
    diff_ref,
    up_ref,
    down_ref,
):
    first_core = jnp.broadcast_to(first_core_ref[...], (ROWS, BLOCK)) > 0
    for b in range(16):
        cols = pl.ds(b * BLOCK, BLOCK)
        even, odd = (mine_ref, other_ref) if b % 2 == 0 else (other_ref, mine_ref)
        coadd = jnp.where(first_core, even[b // 2], odd[b // 2])
        diff_ref[:, cols] = own_ref[:, cols] - coadd
    for q in range(4):
        cols = pl.ds(q * CHUNK, CHUNK)
        down_ref[8 * q : 8 * q + 8, :] = diff_ref[24:32, cols]
        up_ref[8 * q : 8 * q + 8, :] = diff_ref[0:8, cols]
        for extra in range(2):
            at = 32 + 4 * extra + q
            down_ref[at : at + 1, :] = diff_ref[22 + extra : 23 + extra, cols]
            up_ref[at : at + 1, :] = diff_ref[8 + extra : 9 + extra, cols]


def thin_edges(own_ref, row, band_ref, out_ref, frame_ref, halves_ref, done_ref, sems):
    frame = frame_ref[...]
    for part in range(THIN_GROUP):
        moved = pltpu.roll(frame, HALF - part, 1)
        high = moved.astype(BF16).astype(F32)
        spans = jnp.concatenate([high, moved - high, high], axis=0)
        halves_ref[3 * THIN * part : 3 * THIN * (part + 1), :] = spans.astype(BF16)
    used = 3 * THIN * THIN_GROUP
    halves_ref[used:256, :] = jnp.zeros((256 - used, FRAME), BF16)
    width = CHUNK + 128
    copies = []
    for q in range(4):
        cols = pl.ds(q * CHUNK, CHUNK)
        lags = jnp.dot(
            band_ref[...],
            halves_ref[:, q * CHUNK : q * CHUNK + width],
            preferred_element_type=F32,
        )
        total = own_ref[row : row + THIN, cols] + lags[0:THIN, :CHUNK]
        for step in range(1, THIN_STEPS):
            lag = lags[THIN * step : THIN * (step + 1), :]
            total = total + pltpu.roll(lag, width - THIN_GROUP * step, 1)[:, :CHUNK]
        done_ref[:, cols] = total
        copy = pltpu.make_async_copy(
            done_ref.at[:, cols], out_ref.at[pl.ds(row, THIN), cols], sems.at[q]
        )
        copy.start()
        copies.append(copy)
    for copy in copies:
        copy.wait()


def above_kernel(
    own_ref,
    above_ref,
    band_ref,
    out_ref,
    frame_ref,
    halves_ref,
    done_ref,
    sems,
):
    clear(frame_ref, 0)
    put_wide(frame_ref, 8, above_ref, 8)
    for extra in range(2):
        put_thin(frame_ref, 6 + extra, above_ref, 32 + 4 * extra)
    thin_edges(own_ref, 0, band_ref, out_ref, frame_ref, halves_ref, done_ref, sems)


def below_kernel(
    own_ref,
    below_ref,
    band_ref,
    begun_ref,
    out_ref,
    frame_ref,
    halves_ref,
    done_ref,
    sems,
):
    clear(frame_ref, 0)
    put_wide(frame_ref, 0, below_ref, 8)
    for extra in range(2):
        put_thin(frame_ref, 8 + extra, below_ref, 32 + 4 * extra)
    row = ROWS - THIN
    thin_edges(own_ref, row, band_ref, out_ref, frame_ref, halves_ref, done_ref, sems)


def by_lag(kernel):
    return jnp.pad(kernel.T, ((0, 3), (LEAD, SLOT - LEAD - KS)))


def swap(values, step):
    return lax.ppermute(values, "visit", [(i, i ^ step) for i in range(16)])


def over_chips(blocks):
    return lax.all_to_all(
        blocks,
        "visit",
        split_axis=0,
        concat_axis=0,
        axis_index_groups=[list(range(core, 16, 2)) for core in range(2)],
        tiled=True,
    )


def to_next(values):
    return lax.ppermute(values, "row", [(i, (i + 1) % 16) for i in range(16)])


def to_previous(values):
    return lax.ppermute(values, "row", [((i + 1) % 16, i) for i in range(16)])


def on_device(
    science,
    basis_kernels,
    basis_coeffs,
    row_starts,
    row_taps,
    col_offsets,
    col_starts,
    col_taps,
    visit_weights,
    clip_masks,
    decorrelation,
):
    pixels = science[0]
    visit = lax.axis_index("visit")
    band = lax.axis_index("row")
    band_at = band * ROWS
    place = jnp.stack([col_offsets[0], visit % 2, band]).astype(jnp.int32)

    above = to_next(call(down_kernel, sds(72, CHUNK), [VM])(pixels))
    below = to_previous(call(up_kernel, sds(72, CHUNK), [VM])(pixels))

    valid = jnp.stack([band > 0, band < 15]).astype(jnp.int32)
    valid = jnp.broadcast_to(valid[:, None], (2, SLOT))
    first_core = jnp.full((1, BLOCK), visit % 2 == 0).astype(jnp.int32)
    kernel = jnp.einsum(
        "b,bij->ij", basis_coeffs[0], basis_kernels, precision=lax.Precision.HIGHEST
    )
    matched_row = jnp.arange(48, dtype=jnp.int32)[None, :] - 8
    tap_at = matched_row - (jnp.arange(ROWS, dtype=jnp.int32) + row_starts[0])[:, None]
    inside = (matched_row + band_at >= 0) & (matched_row + band_at < 16 * ROWS)
    hits = tap_at[None] == jnp.arange(TAPS, dtype=jnp.int32)[:, None, None]
    mix = jnp.sum(jnp.where(hits & inside[None], row_taps[0][:, :, None], 0.0), axis=0)
    bands = sds(STEPS * ROWS, GROUP * SLOT, dtype=BF16)
    thin_bands = sds(THIN_STEPS * THIN, 256, dtype=BF16)
    own_first, edge_first = call(first_bands_kernel, (bands, bands), [VM] * 3)(
        valid, by_lag(kernel), mix
    )

    frames = [
        pltpu.VMEM((SPAN, FRAME), F32),
        pltpu.VMEM((GROUP * SLOT, FRAME), BF16),
    ]
    own_part = call(own_kernel, sds(ROWS, COLS), [VM] * 2, frames)(pixels, own_first)
    blocks = sds(8, ROWS, BLOCK)
    kept, sent = call(share_kernel, (blocks, blocks), [SM, SM, VM, VM])(
        place, visit_weights, clip_masks[0], col_starts
    )
    shares = kept + swap(sent, 1)
    denominator = jnp.maximum(jnp.sum(over_chips(shares), axis=0), 1.0)
    warped, kept, sent = call(
        warp_kernel,
        (sds(ROWS, COLS), blocks, blocks),
        [ANY, ANY] + [VM] * 7,
        frames
        + [
            pltpu.VMEM((ROWS, LEFT + COLS + 128), F32),
            pltpu.SMEM((3,), jnp.int32),
            pltpu.SMEM((1,), F32),
            pltpu.SemaphoreType.DMA((2,)),
        ],
    )(
        place,
        visit_weights,
        own_part,
        above,
        below,
        edge_first,
        col_starts,
        col_taps[0],
        clip_masks[0],
    )
    sent, denominator = lax.optimization_barrier((sent, denominator))
    second_lags, kept = lax.optimization_barrier((by_lag(decorrelation[0]), kept))
    own_second, above_second, below_second = call(
        second_bands_kernel, (bands, thin_bands, thin_bands), [VM] * 2
    )(valid, second_lags)
    half = kept + swap(sent, 1)
    half, own_second = lax.optimization_barrier((half, own_second))
    coadd = jnp.sum(over_chips(half), axis=0) / denominator
    mine = over_chips(jnp.broadcast_to(coadd[None], (8, ROWS, BLOCK)))
    other = swap(mine, 1)
    difference, up, down = call(
        differ_kernel,
        (sds(ROWS, COLS), sds(40, CHUNK), sds(40, CHUNK)),
        [VM] * 4,
    )(first_core, warped, mine, other)
    above, below = to_next(down), to_previous(up)
    own_part, template = call(
        own_and_template_kernel, (sds(ROWS, COLS), sds(ROWS, BLOCK)), [VM] * 3, frames
    )(difference, own_second, coadd)
    thin_frames = [
        pltpu.VMEM((THIN, FRAME), F32),
        pltpu.VMEM((256, FRAME), BF16),
        pltpu.VMEM((THIN, COLS), F32),
        pltpu.SemaphoreType.DMA((4,)),
    ]
    begun = call(above_kernel, sds(ROWS, COLS), [VM] * 3, thin_frames, ANY)(
        own_part, above, above_second
    )
    cleaned = call(
        below_kernel, sds(ROWS, COLS), [VM] * 3 + [ANY], thin_frames, ANY, {3: 0}
    )(own_part, below, below_second, begun)
    return cleaned[None], template


def solution(mesh):
    return jax.shard_map(
        on_device,
        mesh=mesh,
        in_specs=(
            P("visit", "row", None),
            P(),
            P("visit", None),
            P("visit", "row"),
            P("visit", None, "row"),
            P("visit"),
            P("visit", None),
            P("visit", None, None),
            P("visit"),
            P("visit", "row", None),
            P("visit", None, None),
        ),
        out_specs=(P("visit", "row", None), P("row", "visit")),
        check_vma=False,
    )
```

```python
import jax
import jax.numpy as jnp
from jax import lax
from jax.experimental import pallas as pl
from jax.experimental.pallas import tpu as pltpu
from jax.sharding import PartitionSpec as P

KS = 21
HALF = KS // 2
TAPS = 8
ROWS = 32
COLS = 4096
SPAN = 40
SLOT = 128
BASE = 24
LEAD = 6
CHUNK = 1024
BLOCK = 256
GROUP = 4
STEPS = 6
THIN = 16
THIN_GROUP = 5
THIN_STEPS = 5
FRAME = COLS + 128
LEFT = 640
F32 = jnp.float32
BF16 = jnp.bfloat16
VMEM_LIMIT = 16 * 1024 * 1024

VM = pl.BlockSpec(memory_space=pltpu.VMEM)
SM = pl.BlockSpec(memory_space=pltpu.SMEM)


ANY = pl.BlockSpec(memory_space=pl.ANY)


def call(kernel, outs, ins, scratch=(), places=None, aliases=None):
    return pl.pallas_call(
        kernel,
        out_shape=outs,
        in_specs=ins,
        out_specs=jax.tree.map(lambda _: VM, outs) if places is None else places,
        scratch_shapes=list(scratch),
        input_output_aliases=aliases or {},
        compiler_params=pltpu.CompilerParams(vmem_limit_bytes=VMEM_LIMIT),
    )


def sds(*shape, dtype=F32):
    return jax.ShapeDtypeStruct(shape, dtype)


def down_kernel(x_ref, down_ref):
    for q in range(4):
        cols = pl.ds(q * CHUNK, CHUNK)
        down_ref[16 * q : 16 * q + 16, :] = x_ref[16:32, cols]
        down_ref[64 + q : 65 + q, :] = x_ref[15:16, cols]
        down_ref[68 + q : 69 + q, :] = jnp.zeros((1, CHUNK), F32)


def up_kernel(x_ref, up_ref):
    for q in range(4):
        cols = pl.ds(q * CHUNK, CHUNK)
        up_ref[16 * q : 16 * q + 16, :] = x_ref[0:16, cols]
        up_ref[64 + q : 65 + q, :] = x_ref[16:17, cols]
        up_ref[68 + q : 69 + q, :] = x_ref[17:18, cols]


def between(values, low, high, shift):
    lanes = lax.broadcasted_iota(jnp.int32, values.shape, 1)
    return pltpu.roll(jnp.where((lanes >= low) & (lanes < high), values, 0.0), shift % SLOT, 1)


def put_bands(ref, values):
    lanes = lax.broadcasted_iota(jnp.int32, values.shape, 1)
    spans = values + pltpu.roll(values, SPAN, 1) + pltpu.roll(values, 2 * SPAN, 1)
    high = spans.astype(BF16).astype(F32)
    parts = jnp.where(lanes < 2 * SPAN, high, spans - high).astype(BF16)
    for lag in range(GROUP * STEPS):
        rows = pl.ds(ROWS * (lag // GROUP), ROWS)
        slot = pl.ds(SLOT * (lag % GROUP), SLOT)
        ref[rows, slot] = parts[ROWS * lag : ROWS * (lag + 1)]


def put_thin_bands(ref, values, low, row, valid):
    lanes = lax.broadcasted_iota(jnp.int32, values.shape, 1)
    span = jnp.where(valid, between(values, low, low + THIN, -low), 0.0)
    spans = span + pltpu.roll(span, THIN, 1) + pltpu.roll(span, 2 * THIN, 1)
    high = spans.astype(BF16).astype(F32)
    parts = jnp.where(lanes < 2 * THIN, high, spans - high)
    total = None
    for part in range(THIN_GROUP):
        rows = []
        for step in range(THIN_STEPS):
            at = ROWS * (THIN_GROUP * step + part) + row
            known = at < values.shape[0]
            rows.append(parts[at : at + THIN] if known else jnp.zeros((THIN, SLOT), F32))
        stacked = jnp.concatenate(rows, axis=0)
        wide = jnp.concatenate([stacked, jnp.zeros_like(stacked)], axis=1)
        moved = pltpu.roll(wide, 3 * THIN * part, 1) if part else wide
        total = moved if total is None else total + moved
    ref[...] = total.astype(BF16)


def put_both(own_ref, edge_ref, values, has_above, has_below):
    put_bands(own_ref, between(values, BASE, BASE + ROWS, -BASE))
    above = between(values, BASE - 16, BASE, 16 - BASE)
    above = above + between(values, BASE - 17, BASE - 16, 39 - (BASE - 17))
    below = between(values, BASE + ROWS, BASE + ROWS + 18, 16 - BASE - ROWS)
    put_bands(edge_ref, jnp.where(has_above, above, 0.0) + jnp.where(has_below, below, 0.0))


def skewed(ref, lag, rows, shift):
    values = jnp.broadcast_to(ref[lag : lag + 1, :], (rows, SLOT))
    return pltpu.roll(values, shift, 1, stride=1, stride_axis=0)


def first_bands_kernel(valid_ref, lags_ref, mix_ref, own_ref, edge_ref):
    shape = (ROWS * GROUP * STEPS, SLOT)
    has_above = jnp.broadcast_to(valid_ref[0:1, :], shape) > 0
    has_below = jnp.broadcast_to(valid_ref[1:2, :], shape) > 0
    values = jnp.concatenate([skewed(lags_ref, lag, 48, 0) for lag in range(24)], axis=1)
    merged = jnp.dot(
        mix_ref[...], values, precision=lax.Precision.HIGHEST, preferred_element_type=F32
    )
    slots = [merged[:, SLOT * lag : SLOT * (lag + 1)] for lag in range(24)]
    put_both(own_ref, edge_ref, jnp.concatenate(slots, axis=0), has_above, has_below)


def second_bands_kernel(valid_ref, lags_ref, own_ref, above_ref, below_ref):
    slots = [skewed(lags_ref, lag, ROWS, 8) for lag in range(24)]
    values = jnp.concatenate(slots, axis=0)
    put_bands(own_ref, between(values, BASE, BASE + ROWS, -BASE))
    has_above = jnp.broadcast_to(valid_ref[0:1, :], values.shape) > 0
    has_below = jnp.broadcast_to(valid_ref[1:2, :], values.shape) > 0
    put_thin_bands(above_ref, values, BASE - THIN, 0, has_above)
    put_thin_bands(below_ref, values, BASE + ROWS, ROWS - THIN, has_below)


def coverage(starts, offset, q):
    column = lax.broadcasted_iota(jnp.int32, starts.shape, 1) + q * CHUNK
    actual = column - offset + starts
    return ((actual >= 0) & (actual <= COLS - TAPS)).astype(F32)


def put_blocks(kept_ref, sent_ref, values, first_core, q):
    blocks = [values[:, j * BLOCK : (j + 1) * BLOCK] for j in range(4)]
    for j in range(2):
        even, odd = blocks[2 * j : 2 * j + 2]
        kept_ref[2 * q + j] = jnp.where(first_core, even, odd)
        sent_ref[2 * q + j] = jnp.where(first_core, odd, even)


def share_kernel(
    offset_ref, weight_ref, first_core_ref, mask_ref, starts_ref, kept_ref, sent_ref
):
    first_core = jnp.broadcast_to(first_core_ref[...], (ROWS, BLOCK)) > 0
    for q in range(4):
        cols = pl.ds(q * CHUNK, CHUNK)
        covered = coverage(starts_ref[:, cols], offset_ref[...], q)
        share = weight_ref[...] * mask_ref[:, cols].astype(F32) * covered
        put_blocks(kept_ref, sent_ref, share, first_core, q)


def clear(frame_ref, row):
    rows = frame_ref.shape[0]
    frame_ref[:, COLS:FRAME] = jnp.zeros((rows, FRAME - COLS), F32)
    frame_ref[row:rows, 0:COLS] = jnp.zeros((rows - row, COLS), F32)


def put_wide(frame_ref, row, ref, rows):
    for q in range(4):
        cols = pl.ds(q * CHUNK, CHUNK)
        frame_ref[row : row + rows, cols] = ref[rows * q : rows * (q + 1), :]


def put_thin(frame_ref, row, ref, at):
    for q in range(4):
        frame_ref[row : row + 1, q * CHUNK : (q + 1) * CHUNK] = ref[at + q : at + q + 1, :]


def split_rows(frame_ref, halves_ref):
    frame = frame_ref[...]
    padding = jnp.zeros((SLOT - 3 * SPAN, FRAME), F32)
    for part in range(GROUP):
        moved = pltpu.roll(frame, HALF - part, 1)
        high = moved.astype(BF16).astype(F32)
        spans = jnp.concatenate([high, moved - high, high, padding], axis=0)
        halves_ref[SLOT * part : SLOT * (part + 1), :] = spans.astype(BF16)


def correlate_chunk(band_ref, halves_ref, q):
    width = CHUNK + 128
    lags = jnp.dot(
        band_ref[...],
        halves_ref[:, q * CHUNK : q * CHUNK + width],
        preferred_element_type=F32,
    )
    total = lags[0:ROWS, :CHUNK]
    for step in range(1, STEPS):
        moved = pltpu.roll(lags[ROWS * step : ROWS * (step + 1), :], width - GROUP * step, 1)
        total = total + moved[:, :CHUNK]
    return total


def own_and_template_kernel(
    own_ref, band_ref, coadd_ref, out_ref, template_ref, frame_ref, halves_ref
):
    template_ref[...] = coadd_ref[...]
    own_kernel(own_ref, band_ref, out_ref, frame_ref, halves_ref)


def own_kernel(own_ref, band_ref, out_ref, frame_ref, halves_ref):
    clear(frame_ref, ROWS)
    frame_ref[0:ROWS, 0:COLS] = own_ref[...]
    split_rows(frame_ref, halves_ref)
    for q in range(4):
        out_ref[:, q * CHUNK : (q + 1) * CHUNK] = correlate_chunk(band_ref, halves_ref, q)


def warp_kernel(
    place_source_ref,
    weight_source_ref,
    own_ref,
    above_ref,
    below_ref,
    band_ref,
    starts_ref,
    taps_ref,
    mask_ref,
    warped_ref,
    kept_ref,
    sent_ref,
    frame_ref,
    halves_ref,
    source_ref,
    place_ref,
    weight_ref,
    sems,
):
    fetches = [
        pltpu.make_async_copy(place_source_ref, place_ref, sems.at[0]),
        pltpu.make_async_copy(weight_source_ref, weight_ref, sems.at[1]),
    ]
    for fetch in fetches:
        fetch.start()
    clear(frame_ref, 32)
    put_wide(frame_ref, 0, above_ref, 16)
    put_wide(frame_ref, 16, below_ref, 16)
    put_thin(frame_ref, 32, below_ref, 64)
    put_thin(frame_ref, 33, below_ref, 68)
    put_thin(frame_ref, 39, above_ref, 64)
    split_rows(frame_ref, halves_ref)

    source_ref[:, 0:LEFT] = jnp.zeros((ROWS, LEFT), F32)
    source_ref[:, LEFT + COLS : LEFT + COLS + 128] = jnp.zeros((ROWS, 128), F32)
    for q in range(4):
        edges = correlate_chunk(band_ref, halves_ref, q)
        source_ref[:, LEFT + q * CHUNK : LEFT + (q + 1) * CHUNK] = (
            own_ref[:, q * CHUNK : (q + 1) * CHUNK] + edges
        )

    for fetch in fetches:
        fetch.wait()
    offset = place_ref[0]
    first = LEFT - 3 - offset
    aligned = first // 128
    rest = first - aligned * 128
    width = CHUNK + 256
    for q in range(4):
        cols = pl.ds(q * CHUNK, CHUNK)
        at = pl.multiple_of((aligned + q * (CHUNK // 128)) * 128, 128)
        moved = pltpu.roll(source_ref[:, pl.ds(at, width)], width - rest, 1)
        moved = moved[:, : CHUNK + 128]
        starts = starts_ref[:, cols]
        early = starts == -3
        taps = [taps_ref[t : t + 1, cols] for t in range(TAPS)]
        zero = jnp.zeros_like(taps[0])
        total = None
        for lag in range(TAPS + 1):
            tap = jnp.where(
                early, taps[lag] if lag < TAPS else zero, taps[lag - 1] if lag else zero
            )
            part = moved if lag == 0 else pltpu.roll(moved, CHUNK + 128 - lag, 1)
            term = tap * part[:, :CHUNK]
            total = term if total is None else total + term
        warped_ref[:, cols] = total
        share = weight_ref[0] * mask_ref[:, cols].astype(F32) * coverage(starts, offset, q)
        put_blocks(kept_ref, sent_ref, share * total, place_ref[1] == 0, q)


def differ_kernel(
    first_core_ref,
    own_ref,
    mine_ref,
    other_ref,
    diff_ref,
    up_ref,
    down_ref,
):
    first_core = jnp.broadcast_to(first_core_ref[...], (ROWS, BLOCK)) > 0
    for b in range(16):
        cols = pl.ds(b * BLOCK, BLOCK)
        even, odd = (mine_ref, other_ref) if b % 2 == 0 else (other_ref, mine_ref)
        coadd = jnp.where(first_core, even[b // 2], odd[b // 2])
        diff_ref[:, cols] = own_ref[:, cols] - coadd
    for q in range(4):
        cols = pl.ds(q * CHUNK, CHUNK)
        down_ref[8 * q : 8 * q + 8, :] = diff_ref[24:32, cols]
        up_ref[8 * q : 8 * q + 8, :] = diff_ref[0:8, cols]
        for extra in range(2):
            at = 32 + 4 * extra + q
            down_ref[at : at + 1, :] = diff_ref[22 + extra : 23 + extra, cols]
            up_ref[at : at + 1, :] = diff_ref[8 + extra : 9 + extra, cols]


def thin_edges(own_ref, row, band_ref, out_ref, frame_ref, halves_ref, done_ref, sems):
    frame = frame_ref[...]
    for part in range(THIN_GROUP):
        moved = pltpu.roll(frame, HALF - part, 1)
        high = moved.astype(BF16).astype(F32)
        spans = jnp.concatenate([high, moved - high, high], axis=0)
        halves_ref[3 * THIN * part : 3 * THIN * (part + 1), :] = spans.astype(BF16)
    used = 3 * THIN * THIN_GROUP
    halves_ref[used:256, :] = jnp.zeros((256 - used, FRAME), BF16)
    width = CHUNK + 128
    copies = []
    for q in range(4):
        cols = pl.ds(q * CHUNK, CHUNK)
        lags = jnp.dot(
            band_ref[...],
            halves_ref[:, q * CHUNK : q * CHUNK + width],
            preferred_element_type=F32,
        )
        total = own_ref[row : row + THIN, cols] + lags[0:THIN, :CHUNK]
        for step in range(1, THIN_STEPS):
            lag = lags[THIN * step : THIN * (step + 1), :]
            total = total + pltpu.roll(lag, width - THIN_GROUP * step, 1)[:, :CHUNK]
        done_ref[:, cols] = total
        copy = pltpu.make_async_copy(
            done_ref.at[:, cols], out_ref.at[pl.ds(row, THIN), cols], sems.at[q]
        )
        copy.start()
        copies.append(copy)
    for copy in copies:
        copy.wait()


def above_kernel(
    own_ref,
    above_ref,
    band_ref,
    out_ref,
    frame_ref,
    halves_ref,
    done_ref,
    sems,
):
    clear(frame_ref, 0)
    put_wide(frame_ref, 8, above_ref, 8)
    for extra in range(2):
        put_thin(frame_ref, 6 + extra, above_ref, 32 + 4 * extra)
    thin_edges(own_ref, 0, band_ref, out_ref, frame_ref, halves_ref, done_ref, sems)


def below_kernel(
    own_ref,
    below_ref,
    band_ref,
    begun_ref,
    out_ref,
    frame_ref,
    halves_ref,
    done_ref,
    sems,
):
    clear(frame_ref, 0)
    put_wide(frame_ref, 0, below_ref, 8)
    for extra in range(2):
        put_thin(frame_ref, 8 + extra, below_ref, 32 + 4 * extra)
    row = ROWS - THIN
    thin_edges(own_ref, row, band_ref, out_ref, frame_ref, halves_ref, done_ref, sems)


def by_lag(kernel):
    return jnp.pad(kernel.T, ((0, 3), (LEAD, SLOT - LEAD - KS)))


def swap(values, step):
    return lax.ppermute(values, "visit", [(i, i ^ step) for i in range(16)])


def over_chips(blocks):
    return lax.all_to_all(
        blocks,
        "visit",
        split_axis=0,
        concat_axis=0,
        axis_index_groups=[list(range(core, 16, 2)) for core in range(2)],
        tiled=True,
    )


def to_next(values):
    return lax.ppermute(values, "row", [(i, (i + 1) % 16) for i in range(16)])


def to_previous(values):
    return lax.ppermute(values, "row", [((i + 1) % 16, i) for i in range(16)])


def on_device(
    science,
    basis_kernels,
    basis_coeffs,
    row_starts,
    row_taps,
    col_offsets,
    col_starts,
    col_taps,
    visit_weights,
    clip_masks,
    decorrelation,
):
    pixels = science[0]
    visit = lax.axis_index("visit")
    band = lax.axis_index("row")
    band_at = band * ROWS
    place = jnp.stack([col_offsets[0], visit % 2, band]).astype(jnp.int32)

    above = to_next(call(down_kernel, sds(72, CHUNK), [VM])(pixels))
    below = to_previous(call(up_kernel, sds(72, CHUNK), [VM])(pixels))

    valid = jnp.stack([band > 0, band < 15]).astype(jnp.int32)
    valid = jnp.broadcast_to(valid[:, None], (2, SLOT))
    first_core = jnp.full((1, BLOCK), visit % 2 == 0).astype(jnp.int32)
    kernel = jnp.einsum(
        "b,bij->ij", basis_coeffs[0], basis_kernels, precision=lax.Precision.HIGHEST
    )
    matched_row = jnp.arange(48, dtype=jnp.int32)[None, :] - 8
    tap_at = matched_row - (jnp.arange(ROWS, dtype=jnp.int32) + row_starts[0])[:, None]
    inside = (matched_row + band_at >= 0) & (matched_row + band_at < 16 * ROWS)
    hits = tap_at[None] == jnp.arange(TAPS, dtype=jnp.int32)[:, None, None]
    mix = jnp.sum(jnp.where(hits & inside[None], row_taps[0][:, :, None], 0.0), axis=0)
    bands = sds(STEPS * ROWS, GROUP * SLOT, dtype=BF16)
    thin_bands = sds(THIN_STEPS * THIN, 256, dtype=BF16)
    own_first, edge_first = call(first_bands_kernel, (bands, bands), [VM] * 3)(
        valid, by_lag(kernel), mix
    )

    frames = [
        pltpu.VMEM((SPAN, FRAME), F32),
        pltpu.VMEM((GROUP * SLOT, FRAME), BF16),
    ]
    own_part = call(own_kernel, sds(ROWS, COLS), [VM] * 2, frames)(pixels, own_first)
    blocks = sds(8, ROWS, BLOCK)
    kept, sent = call(share_kernel, (blocks, blocks), [VM] * 5)(
        col_offsets[None], visit_weights[None], first_core, clip_masks[0], col_starts
    )
    shares = kept + swap(sent, 1)
    denominator = jnp.maximum(jnp.sum(over_chips(shares), axis=0), 1.0)
    warped, kept, sent = call(
        warp_kernel,
        (sds(ROWS, COLS), blocks, blocks),
        [ANY, ANY] + [VM] * 7,
        frames
        + [
            pltpu.VMEM((ROWS, LEFT + COLS + 128), F32),
            pltpu.SMEM((3,), jnp.int32),
            pltpu.SMEM((1,), F32),
            pltpu.SemaphoreType.DMA((2,)),
        ],
    )(
        place,
        visit_weights,
        own_part,
        above,
        below,
        edge_first,
        col_starts,
        col_taps[0],
        clip_masks[0],
    )
    sent, denominator = lax.optimization_barrier((sent, denominator))
    second_lags, kept = lax.optimization_barrier((by_lag(decorrelation[0]), kept))
    own_second, above_second, below_second = call(
        second_bands_kernel, (bands, thin_bands, thin_bands), [VM] * 2
    )(valid, second_lags)
    half = kept + swap(sent, 1)
    half, own_second = lax.optimization_barrier((half, own_second))
    coadd = jnp.sum(over_chips(half), axis=0) / denominator
    mine = over_chips(jnp.broadcast_to(coadd[None], (8, ROWS, BLOCK)))
    other = swap(mine, 1)
    difference, up, down = call(
        differ_kernel,
        (sds(ROWS, COLS), sds(40, CHUNK), sds(40, CHUNK)),
        [VM] * 4,
    )(first_core, warped, mine, other)
    above, below = to_next(down), to_previous(up)
    own_part, template = call(
        own_and_template_kernel, (sds(ROWS, COLS), sds(ROWS, BLOCK)), [VM] * 3, frames
    )(difference, own_second, coadd)
    thin_frames = [
        pltpu.VMEM((THIN, FRAME), F32),
        pltpu.VMEM((256, FRAME), BF16),
        pltpu.VMEM((THIN, COLS), F32),
        pltpu.SemaphoreType.DMA((4,)),
    ]
    begun = call(above_kernel, sds(ROWS, COLS), [VM] * 3, thin_frames, ANY)(
        own_part, above, above_second
    )
    cleaned = call(
        below_kernel, sds(ROWS, COLS), [VM] * 3 + [ANY], thin_frames, ANY, {3: 0}
    )(own_part, below, below_second, begun)
    return cleaned[None], template


def solution(mesh):
    return jax.shard_map(
        on_device,
        mesh=mesh,
        in_specs=(
            P("visit", "row", None),
            P(),
            P("visit", None),
            P("visit", "row"),
            P("visit", None, "row"),
            P("visit"),
            P("visit", None),
            P("visit", None, None),
            P("visit"),
            P("visit", "row", None),
            P("visit", None, None),
        ),
        out_specs=(P("visit", "row", None), P("row", "visit")),
        check_vma=False,
    )
```
